128 devices in a mesh: dp: 8 (over x, core), tensor: 16 (over z, y).
Axes of the slice: x: 4, y: 4, z: 4, core: 2. Of those that a mesh axis runs over, the one named last changes fastest.
Arguments:
- tokens: bfloat16 [3072, 4096], P('dp', 'tensor'), may hold values from -6 to 6
- gate_weight_codes: bfloat16 [4096, 14336], P(None, 'tensor')
- up_weight_codes: bfloat16 [4096, 14336], P(None, 'tensor')
- down_weight_codes: bfloat16 [14336, 4096], P('tensor')
- gate_channel_scale: float32 [14336], P('tensor'), may hold values from 0.0001 to 0.0004
- up_channel_scale: float32 [14336], P('tensor'), may hold values from 0.0001 to 0.0004
- down_channel_scale: float32 [4096], P('tensor'), may hold values from 0.0001 to 0.0004
- adapter_input_factors: bfloat16 [4096, 1024], P(None, 'dp'), may hold values from -0.09375 to 0.09375
- adapter_output_factors: bfloat16 [14336, 1024], P('tensor', 'dp'), may hold values from -0.8984375 to 0.8984375
- group_adapter_lists: int32 [8, 8, 2], replicated, may hold values from -1 to 7, as said below
- row_adapter_entry: int32 [3072], P('dp'), may hold values from 0 to 15, as said below
Outputs:
- mixed: bfloat16 [3072, 4096], P('dp', 'tensor')
The draws below stay inside these ranges and needn't reach their ends.
Inputs may be any that keep to these rules, and one draw needn't show every extreme that they name: `group_adapter_lists`: entry (g, o, s) is the index, among the 8 adapters that owner group o holds, of the s-th adapter that group g takes from o, or -1 for an unused slot. Filled slots of a pair come first and name different adapters. Every group has a filled slot, and in every draw some group fills all 2 slots from every owner. Row r of group g = r // 384 reads owner o = row_adapter_entry // 2 and slot s = row_adapter_entry % 2; group_adapter_lists[g, o, s] is always filled.
All inputs are finite; a program needn't handle non-finite values.
Results may differ from the reference program's by a relative error of at most 0.0059.
Values may be sent and summed in bfloat16 or wider, within the bound.
A program may use at most 128 MiB of HBM per device.

```python
import math
import jax
import jax.numpy as jnp
from jax import lax

MODEL_WIDTH = 4096
PALEY = 28
WALSH = 512
HIDDEN_UNITS = 14336
ADAPTER_RANK = 16
ADPT_DEV = 8
SLOT = 2
ROW_DEV = 384
ROWS = 3072
ADAPTER_TOTAL = 64
N_DP = 8


def adapter_layout(key):
    folded = jax.random.fold_in(key, 11)
    first_key, second_key, third_key, fourth_key = jax.random.split(folded, 4)
    counts = jax.random.randint(first_key, (N_DP, N_DP), 0, SLOT + 1)
    anchor = jax.random.randint(second_key, (N_DP,), 0, N_DP)
    owners = jnp.arange(N_DP)
    counts = jnp.where(owners[None, :] == anchor[:, None], jnp.maximum(counts, 1), counts)
    full_group = jax.random.randint(third_key, (), 0, N_DP)
    counts = jnp.where(owners[:, None] == full_group, SLOT, counts)
    pair_keys = jax.random.split(fourth_key, N_DP * N_DP)
    orders = jax.vmap(lambda single: jax.random.permutation(single, ADPT_DEV))(pair_keys)
    orders = orders.reshape(N_DP, N_DP, ADPT_DEV)[:, :, :SLOT]
    places = jnp.arange(SLOT)
    return jnp.where(places[None, None, :] < counts[:, :, None], orders, -1).astype(jnp.int32)


def draw_group_adapter_lists(key, part):
    return adapter_layout(key)


def draw_row_adapter_entry(key, part):
    table = adapter_layout(key)
    key = jax.random.fold_in(key, 5)
    filled = (table >= 0).reshape(N_DP, N_DP * SLOT).astype(jnp.int32)
    totals = jnp.sum(filled, axis=1)
    group = jnp.arange(ROWS) // ROW_DEV
    wanted = jax.random.randint(key, (ROWS,), 0, totals[group])
    ranks = jnp.cumsum(filled, axis=1) - 1
    target = (filled[group] == 1) & (ranks[group] == wanted[:, None])
    return jnp.sum(target.astype(jnp.int32) * jnp.arange(N_DP * SLOT)[None, :], axis=1).astype(jnp.int32)


def draw_gate_weight_codes(key, part):
    key = jax.random.fold_in(key, 1)
    return jax.random.randint(key, (MODEL_WIDTH, HIDDEN_UNITS), -127, 128).astype(jnp.float32).astype(jnp.bfloat16)


def draw_up_weight_codes(key, part):
    key = jax.random.fold_in(key, 2)
    return jax.random.randint(key, (MODEL_WIDTH, HIDDEN_UNITS), -127, 128).astype(jnp.float32).astype(jnp.bfloat16)


def draw_down_weight_codes(key, part):
    key = jax.random.fold_in(key, 3)
    return jax.random.randint(key, (HIDDEN_UNITS, MODEL_WIDTH), -127, 128).astype(jnp.float32).astype(jnp.bfloat16)


def block_scale(key, dims, shards, low, largest):
    def one(axis_at, shards_of):
        draws = jax.random.uniform(jax.random.fold_in(jax.random.fold_in(key, 6), axis_at), (shards_of,), jnp.float32, low / len(shards), largest / len(shards))
        return jnp.repeat(jnp.exp(draws), dims[axis_at] // shards_of).reshape((-1,) + (1,) * (len(dims) - axis_at - 1))

    gain = one(*shards[0])
    for cut in shards[1:]:
        gain = gain * one(*cut)
    return gain


def scatter_about(own_key, dims, deviation, most, cuts=(), held_as=jnp.bfloat16):
    array = deviation * jax.random.normal(own_key, dims, jnp.float32)
    if cuts:
        array = array * block_scale(own_key, dims, cuts, -0.22, 0.18)
    return jnp.clip(array, -most, most).astype(held_as)


def setup_inputs(seed: int = 0) -> dict:
    seeds = jax.random.split(jax.random.key(seed), 12)
    return {
        "tokens": scatter_about(seeds[0], (ROWS, MODEL_WIDTH), 1.0, 6.0, ((0, 8), (1, 16))),
        "gate_weight_codes": draw_gate_weight_codes(jax.random.fold_in(seeds[11], 71), 0),
        "up_weight_codes": draw_up_weight_codes(jax.random.fold_in(seeds[11], 71), 0),
        "down_weight_codes": draw_down_weight_codes(jax.random.fold_in(seeds[11], 71), 0),
        "gate_channel_scale": jnp.clip(jnp.exp(math.log(0.0004) - 1.3862944 * jax.random.uniform(seeds[4], (HIDDEN_UNITS,), jnp.float32) ** block_scale(seeds[4], (HIDDEN_UNITS,), ((0, 16),), -0.2, 0.2)), 0.0001, 0.0004),
        "up_channel_scale": jnp.clip(jnp.exp(math.log(0.0004) - 1.3862944 * jax.random.uniform(seeds[5], (HIDDEN_UNITS,), jnp.float32) ** block_scale(seeds[5], (HIDDEN_UNITS,), ((0, 16),), -0.2, 0.2)), 0.0001, 0.0004),
        "down_channel_scale": jnp.clip(jnp.exp(math.log(0.0004) - 1.3862944 * jax.random.uniform(seeds[6], (MODEL_WIDTH,), jnp.float32) ** block_scale(seeds[6], (MODEL_WIDTH,), ((0, 16),), -0.2, 0.2)), 0.0001, 0.0004),
        "adapter_input_factors": scatter_about(seeds[7], (MODEL_WIDTH, ADAPTER_TOTAL * ADAPTER_RANK), MODEL_WIDTH ** -0.5, 0.09375, ((1, 8),)),
        "adapter_output_factors": scatter_about(seeds[8], (HIDDEN_UNITS, ADAPTER_TOTAL * ADAPTER_RANK), 0.15, 0.8984375, ((0, 16), (1, 8))),
        "group_adapter_lists": draw_group_adapter_lists(jax.random.fold_in(seeds[11], 71), 0),
        "row_adapter_entry": draw_row_adapter_entry(jax.random.fold_in(seeds[11], 71), 0),
    }


def sylvester_table(order):
    first = jnp.arange(order, dtype=jnp.int32)[:, None]
    second = jnp.arange(order, dtype=jnp.int32)[None, :]
    common = first & second
    parity = jnp.zeros((order, order), jnp.int32)
    for bit_number in range(max(order.bit_length() - 1, 0)):
        parity = parity + (common >> bit_number & 1)
    return (1 - 2 * (parity % 2)).astype(jnp.float32)

def paley_table():
    index = jnp.arange(28, dtype=jnp.int32)
    outer_index = index // 2
    inner_index = index % 2
    left = outer_index[:, None]
    right = outer_index[None, :]
    offset = (right - left) % 13
    square = (offset == 1) | (offset == 3) | (offset == 4) | (offset == 9) | (offset == 10) | (offset == 12)
    legendre = jnp.where(offset == 0, 0.0, jnp.where(square, 1.0, -1.0))
    edge = (left == 0) | (right == 0)
    corner = (left == 0) & (right == 0)
    conference = jnp.where(corner, 0.0, jnp.where(edge, 1.0, legendre)).astype(jnp.float32)
    low_row = inner_index[:, None]
    low_col = inner_index[None, :]
    first_block = jnp.where((low_row == 1) & (low_col == 1), -1.0, 1.0).astype(jnp.float32)
    second_block = jnp.where((low_row == 0) & (low_col == 0), 1.0, -1.0).astype(jnp.float32)
    diagonal = (left == right).astype(jnp.float32)
    return conference * first_block + diagonal * second_block

def reference(tokens, gate_weight_codes, up_weight_codes, down_weight_codes, gate_channel_scale, up_channel_scale, down_channel_scale, adapter_input_factors, adapter_output_factors, group_adapter_lists, row_adapter_entry):
    group = (jnp.arange(ROWS) // ROW_DEV).astype(jnp.int32)
    owner = (row_adapter_entry // SLOT).astype(jnp.int32)
    place = (row_adapter_entry % SLOT).astype(jnp.int32)
    adapter = owner * ADPT_DEV + group_adapter_lists[group, owner, place]
    gate = jnp.dot(tokens, gate_weight_codes, preferred_element_type=jnp.float32) * gate_channel_scale
    low_rank_everyall = jnp.dot(tokens, adapter_input_factors, preferred_element_type=jnp.float32)
    column_block = (jnp.arange(ADAPTER_TOTAL * ADAPTER_RANK) // ADAPTER_RANK).astype(jnp.int32)
    keep = column_block[None, :] == adapter[:, None]
    low_rank_rows = jnp.where(keep, low_rank_everyall, jnp.zeros_like(low_rank_everyall)).astype(jnp.bfloat16)
    adapter_extra = lax.dot_general(low_rank_rows, adapter_output_factors, (((1,), (1,)), ((), ())), preferred_element_type=jnp.float32)
    up = jnp.dot(tokens, up_weight_codes, preferred_element_type=jnp.float32) * up_channel_scale + adapter_extra
    hidden = (jax.nn.silu(gate) * up).astype(jnp.bfloat16)
    blocks = hidden.astype(jnp.float32).reshape(ROWS, WALSH, PALEY)
    inner = jnp.einsum('rwa,ab->rwb', blocks, paley_table(), precision=lax.Precision.HIGHEST)
    outer = jnp.einsum('rwb,wv->rvb', inner, sylvester_table(WALSH), precision=lax.Precision.HIGHEST)
    rotated = (outer.reshape(ROWS, HIDDEN_UNITS) / math.sqrt(HIDDEN_UNITS)).astype(jnp.bfloat16)
    summed = jnp.dot(rotated, down_weight_codes, preferred_element_type=jnp.float32)
    return (summed * down_channel_scale).astype(jnp.bfloat16)
```

```python
import functools
import math

import jax
import jax.numpy as jnp
import numpy as np
from jax import lax
from jax.experimental import pallas as pl
from jax.experimental.pallas import tpu as pltpu
from jax.sharding import PartitionSpec as P

HIDDEN_UNITS = 14336
RANK = 16
SIDE = 4
TENSOR = SIDE * SIDE
GROUPS = 8
SLOTS = 2
QUARTERS = 4
MIB = 1024 * 1024


def steps(a):
    return min(a, SIDE - a)


def depth(o):
    return steps(o[0]) + steps(o[1])


OFFSETS = sorted(((a, b) for a in range(SIDE) for b in range(SIDE)), key=depth)
ORDER = {o: i for i, o in enumerate(OFFSETS)}


def parent(q, o):
    dz, dy = o
    via = 1 if q % 2 == 0 else SIDE - 1

    def back(a):
        return via if a == 2 else 0

    if q < 2:
        return (dz, back(dy)) if dy else (back(dz), 0)
    return (back(dz), dy) if dz else (0, back(dy))


CHILDREN = {
    (q, o): [c for c in OFFSETS if c != (0, 0) and parent(q, c) == o]
    for q in range(QUARTERS)
    for o in OFFSETS
}


def rotation_table(local_units):
    order = local_units // 28
    index = np.arange(order)
    walsh = np.ones((order, order), np.int64)
    for bit in range(max(order.bit_length() - 1, 0)):
        walsh *= 1 - 2 * ((index[:, None] & index[None, :]) >> bit & 1)
    conference = np.ones((14, 14), np.int64)
    residues = {j * j % 13 for j in range(1, 13)}
    conference[0, 0] = 0
    for i in range(13):
        for j in range(13):
            offset = (j - i) % 13
            conference[i + 1, j + 1] = 0 if offset == 0 else (1 if offset in residues else -1)
    paley = np.kron(conference, np.array([[1, 1], [1, -1]])) + np.kron(
        np.eye(14, dtype=np.int64), np.array([[1, -1], [-1, -1]])
    )
    return np.kron(walsh, paley).astype(np.float32)


def body(
    tokens, wg, wu, wd, gs, us, ds, fa, fb, lists, entry, table, out,
    xs, wv, wdv, tv, acc, hid, gst, ra, rb, rot, rotc, part, rss, rsr,
    fav, fbv, stage, fac, lrz, lry, low,
    own_sem, w_sem, misc_sem, ag_s, ag_r, dp_s, dp_r, lz_s, lz_r, ly_s, ly_r,
    a1_s, a1_r, a2_s, a2_r, rs_s, rs_r,
):
    rows, width = tokens.shape
    units = wg.shape[1]
    quarter = rows // QUARTERS
    panels = units // 128
    share = ra.shape[1]
    d = lax.axis_index("dp")
    t = lax.axis_index("tensor")
    z = lax.div(t, SIDE)
    y = lax.rem(t, SIDE)

    def at(o, sign=1):
        return (
            lax.rem(z + sign * o[0] + SIDE, SIDE) * SIDE + lax.rem(y + sign * o[1] + SIDE, SIDE)
        )

    def remote(src, dst, send, recv, to, axis="tensor"):
        return pltpu.make_async_remote_copy(
            src_ref=src, dst_ref=dst, send_sem=send, recv_sem=recv,
            device_id={axis: to}, device_id_type=pl.DeviceIdType.MESH,
        )

    sent = []

    def send(*args, **kw):
        copy = remote(*args, **kw)
        copy.start()
        sent.append(copy)

    barrier = pltpu.get_barrier_semaphore()
    for o in OFFSETS[1:]:
        pl.semaphore_signal(
            barrier, inc=1, device_id={"tensor": at(o)}, device_id_type=pl.DeviceIdType.MESH
        )
    for i in range(1, GROUPS):
        pl.semaphore_signal(
            barrier, inc=1, device_id={"dp": lax.rem(d + i, GROUPS)},
            device_id_type=pl.DeviceIdType.MESH,
        )

    own = pltpu.make_async_copy(tokens, xs.at[t], own_sem)
    own.start()
    fa_copy = pltpu.make_async_copy(
        fa.at[pl.ds(pl.multiple_of(t * width, width), width), :], fav, misc_sem.at[0]
    )
    fa_copy.start()
    fb_copy = pltpu.make_async_copy(fb, fbv, misc_sem.at[1])
    fb_copy.start()
    w_copies = []
    for i, o in enumerate(OFFSETS):
        block = pl.ds(pl.multiple_of(at(o, -1) * width, width), width)
        pair = (
            pltpu.make_async_copy(wg.at[block, :], wv.at[i, :, 0:units], w_sem.at[i, 0]),
            pltpu.make_async_copy(wu.at[block, :], wv.at[i, :, units : 2 * units], w_sem.at[i, 1]),
        )
        for copy in pair:
            copy.start()
        w_copies.append(pair)
    table_copy = pltpu.make_async_copy(table, tv, misc_sem.at[2])
    table_copy.start()
    wd_copy = pltpu.make_async_copy(wd, wdv, misc_sem.at[3])
    wd_copy.start()

    fa_copy.wait()
    fb_copy.wait()
    rank_row = lax.broadcasted_iota(jnp.int32, (RANK, GROUPS * RANK), 0)
    column = lax.broadcasted_iota(jnp.int32, (RANK, GROUPS * RANK), 1)
    picks = []
    for g in range(GROUPS):
        for s in range(SLOTS):
            picked = lists[g * GROUPS * SLOTS + d * SLOTS + s]
            picks.append((column == picked * RANK + rank_row).astype(jnp.float32))
    pick = jnp.concatenate(picks, axis=0).astype(jnp.bfloat16)
    nt = (((1,), (1,)), ((), ()))
    stage[:, 0:width] = lax.dot_general(
        pick, fav[...], nt, preferred_element_type=jnp.float32
    ).astype(jnp.bfloat16)
    stage[:, width:] = lax.dot_general(
        pick, fbv[...], nt, preferred_element_type=jnp.float32
    ).astype(jnp.bfloat16)
    block_rows = SLOTS * RANK
    mine = pl.ds(pl.multiple_of(d * block_rows, block_rows), block_rows)
    fac[mine, :] = stage[mine, :]

    pl.semaphore_wait(barrier, TENSOR - 1 + GROUPS - 1)

    def rows_of(q):
        return pl.ds(q * quarter, quarter)

    def forward(q, o):
        source = at(o, -1)
        for c in CHILDREN[q, o]:
            hop = (c[0] - o[0], c[1] - o[1])
            src = tokens.at[rows_of(q), :] if o == (0, 0) else xs.at[source, rows_of(q), :]
            send(
                src, xs.at[source, rows_of(q), :],
                ag_s.at[q, ORDER[c]], ag_r.at[q, ORDER[c]], at(hop),
            )

    def arrived(q, o):
        source = at(o, -1)
        slot = xs.at[source, rows_of(q), :]
        remote(slot, slot, ag_s.at[q, ORDER[o]], ag_r.at[q, ORDER[o]], source).wait_recv()

    def multiply(i, o):
        source = at(o, -1)
        for copy in w_copies[i]:
            copy.wait()

        @pl.loop(0, 2 * units // 256)
        def _(n):
            columns = pl.ds(pl.multiple_of(n * 256, 256), 256)
            product = jnp.dot(
                xs[source], wv[i, :, columns], preferred_element_type=jnp.float32
            )
            if i == 0:
                acc[:, columns] = product
            else:
                acc[:, columns] += product

    for q in range(QUARTERS):
        forward(q, (0, 0))
    for i in range(1, GROUPS):
        peer = lax.rem(d + i, GROUPS)
        theirs = pl.ds(pl.multiple_of(peer * block_rows, block_rows), block_rows)
        send(stage.at[theirs, :], fac.at[mine, :], dp_s.at[i], dp_r.at[i], peer, axis="dp")
    own.wait()
    multiply(0, (0, 0))

    slot_of = lax.broadcasted_iota(jnp.int32, (GROUPS * SLOTS * RANK, rows), 0) // RANK
    chosen = slot_of == entry[...]

    def low_partial():
        for i in range(1, GROUPS):
            peer = lax.rem(d - i + GROUPS, GROUPS)
            theirs = pl.ds(pl.multiple_of(peer * block_rows, block_rows), block_rows)
            slot = fac.at[theirs, :]
            remote(slot, slot, dp_s.at[i], dp_r.at[i], peer, axis="dp").wait_recv()
        everyone = lax.dot_general(
            fac[:, 0:width], xs[t], nt, preferred_element_type=jnp.float32
        )
        kept = jnp.where(chosen, everyone, 0.0)
        lrz[0] = jnp.sum(kept.reshape(GROUPS * SLOTS, RANK, rows), axis=0)
        for i in range(1, SIDE):
            send(lrz.at[0], lrz.at[i], lz_s.at[i], lz_r.at[i], at((i, 0)))

    def low_along_y():
        for i in range(1, SIDE):
            remote(lrz.at[i], lrz.at[i], lz_s.at[i], lz_r.at[i], at((i, 0), -1)).wait_recv()
        lry[0] = (lrz[0] + lrz[1]) + (lrz[2] + lrz[3])
        for i in range(1, SIDE):
            send(lry.at[0], lry.at[i], ly_s.at[i], ly_r.at[i], at((0, i)))

    def low_whole():
        for i in range(1, SIDE):
            remote(lry.at[i], lry.at[i], ly_s.at[i], ly_r.at[i], at((0, i), -1)).wait_recv()
        total = (lry[0] + lry[1]) + (lry[2] + lry[3])
        total = total.astype(jnp.bfloat16).astype(jnp.float32)
        spread = jnp.concatenate([total] * (GROUPS * SLOTS), axis=0)
        low[...] = jnp.transpose(jnp.where(chosen, spread, 0.0)).astype(jnp.bfloat16)

    after = {4: low_partial, 10: low_along_y, 14: low_whole}
    for i, o in enumerate(OFFSETS):
        if i == 0:
            continue
        for q in range(QUARTERS):
            arrived(q, o)
            forward(q, o)
        multiply(i, o)
        if i in after:
            after[i]()

    @pl.loop(0, panels)
    def _(j):
        columns = pl.ds(pl.multiple_of(j * 128, 128), 128)
        up_columns = pl.ds(pl.multiple_of(units + j * 128, 128), 128)
        factor_columns = pl.ds(pl.multiple_of(width + j * 128, 128), 128)
        gate = acc[:, columns] * gs[:, columns]
        extra = jnp.dot(low[...], fac[:, factor_columns], preferred_element_type=jnp.float32)
        up = acc[:, up_columns] * us[:, columns] + extra
        hid[:, columns] = (gate / (1.0 + jnp.exp(-gate)) * up).astype(jnp.bfloat16)

    table_copy.wait()
    for j in range(0, panels, 2):
        wide = min(2, panels - j)
        turned = jnp.dot(
            hid[...], tv[:, j * 128 : (j + wide) * 128], preferred_element_type=jnp.float32
        ).astype(jnp.bfloat16)
        for k in range(wide):
            gst[(j + k) * rows : (j + k + 1) * rows, :] = turned[:, k * 128 : (k + 1) * 128]
    gst[panels * rows :, :] = jnp.zeros((gst.shape[0] - panels * rows, 128), jnp.bfloat16)

    def share_of(index):
        return pl.ds(pl.multiple_of(index * share, 16), share)

    far_first = OFFSETS[:0:-1]
    for o in far_first:
        i = ORDER[o]
        peer = at(o)
        send(gst.at[share_of(peer), :], ra.at[t], a1_s.at[i], a1_r.at[i], peer)
    ra[t] = gst[share_of(t), :]
    for o in far_first[::-1]:
        i = ORDER[o]
        peer = at(o, -1)
        remote(ra.at[peer], ra.at[peer], a1_s.at[i], a1_r.at[i], peer).wait_recv()
    norm = 1.0 / math.sqrt(HIDDEN_UNITS)

    @pl.loop(0, share // 16)
    def _(k):
        tile = pl.ds(pl.multiple_of(k * 16, 16), 16)
        terms = [ra[i, tile, :].astype(jnp.float32) for i in range(TENSOR)]
        for bit in range(4):
            mixed = list(terms)
            for i in range(TENSOR):
                j = i ^ (1 << bit)
                if i < j:
                    mixed[i] = terms[i] + terms[j]
                    mixed[j] = terms[i] - terms[j]
            terms = mixed
        for i in range(TENSOR):
            rb[i, tile, :] = (terms[i] * norm).astype(jnp.bfloat16)

    for o in far_first:
        i = ORDER[o]
        peer = at(o)
        send(rb.at[peer], rot.at[share_of(t), :], a2_s.at[i], a2_r.at[i], peer)
    rot[share_of(t), :] = rb[t]
    for o in far_first[::-1]:
        i = ORDER[o]
        peer = at(o, -1)
        slot = rot.at[share_of(peer), :]
        remote(slot, slot, a2_s.at[i], a2_r.at[i], peer).wait_recv()
    for j in range(panels):
        rotc[:, j * 128 : (j + 1) * 128] = rot[j * rows : (j + 1) * rows, :]

    wd_copy.wait()

    def project(o):
        target = at(o, -1)
        columns = pl.ds(pl.multiple_of(target * width, width), width)
        part[ORDER[o]] = jnp.dot(
            rotc[...], wdv[:, columns], preferred_element_type=jnp.float32
        )

    def collected(q, o):
        total = part[ORDER[o], rows_of(q), :]
        for c in CHILDREN[q, o]:
            slot = rsr.at[ORDER[c], rows_of(q), :]
            remote(slot, slot, rs_s.at[q, ORDER[c]], rs_r.at[q, ORDER[c]], t).wait_recv()
            total = total + rsr[ORDER[c], rows_of(q), :].astype(jnp.float32)
        return total

    def pass_up(q, o):
        rss[ORDER[o], rows_of(q), :] = collected(q, o).astype(jnp.bfloat16)
        above = parent(q, o)
        hop = (above[0] - o[0], above[1] - o[1])
        send(
            rss.at[ORDER[o], rows_of(q), :], rsr.at[ORDER[o], rows_of(q), :],
            rs_s.at[q, ORDER[o]], rs_r.at[q, ORDER[o]], at(hop),
        )

    for level in (4, 3, 2, 1):
        here = [o for o in OFFSETS if depth(o) == level]
        for o in here:
            project(o)
            for q in range(QUARTERS):
                if not CHILDREN[q, o]:
                    pass_up(q, o)
        if level == 1:
            project((0, 0))
        for o in here:
            for q in range(QUARTERS):
                if CHILDREN[q, o]:
                    pass_up(q, o)
    for q in range(QUARTERS):
        out[rows_of(q), :] = (collected(q, (0, 0)) * ds[...]).astype(jnp.bfloat16)
    for copy in sent:
        copy.wait_send()


def local(
    tokens,
    gate_weight_codes,
    up_weight_codes,
    down_weight_codes,
    gate_channel_scale,
    up_channel_scale,
    down_channel_scale,
    adapter_input_factors,
    adapter_output_factors,
    group_adapter_lists,
    row_adapter_entry,
):
    rows, width = tokens.shape
    units = gate_weight_codes.shape[1]
    factors = adapter_input_factors.shape[1]
    picked = GROUPS * SLOTS * RANK
    panels = units // 128
    share = -(-panels * rows // (16 * TENSOR)) * 16
    bf16, f32 = jnp.bfloat16, jnp.float32
    table = jnp.asarray(rotation_table(units), bf16)
    hbm = pl.BlockSpec(memory_space=pl.ANY)
    vmem = pl.BlockSpec(memory_space=pltpu.VMEM)
    smem = pl.BlockSpec(memory_space=pltpu.SMEM)
    dma = pltpu.SemaphoreType.DMA
    return pl.pallas_call(
        body,
        out_shape=jax.ShapeDtypeStruct((rows, width), bf16),
        in_specs=[hbm, hbm, hbm, hbm, vmem, vmem, vmem, hbm, hbm, smem, vmem, hbm],
        out_specs=vmem,
        scratch_shapes=[
            pltpu.VMEM((TENSOR, rows, width), bf16),
            pltpu.VMEM((TENSOR, width, 2 * units), bf16),
            pltpu.VMEM(down_weight_codes.shape, bf16),
            pltpu.VMEM((units, units), bf16),
            pltpu.VMEM((rows, 2 * units), f32),
            pltpu.VMEM((rows, units), bf16),
            pltpu.VMEM((TENSOR * share, 128), bf16),
            pltpu.VMEM((TENSOR, share, 128), bf16),
            pltpu.VMEM((TENSOR, share, 128), bf16),
            pltpu.VMEM((TENSOR * share, 128), bf16),
            pltpu.VMEM((rows, units), bf16),
            pltpu.VMEM((TENSOR, rows, width), f32),
            pltpu.VMEM((TENSOR, rows, width), bf16),
            pltpu.VMEM((TENSOR, rows, width), bf16),
            pltpu.VMEM((width, factors), bf16),
            pltpu.VMEM((units, factors), bf16),
            pltpu.VMEM((picked, width + units), bf16),
            pltpu.VMEM((picked, width + units), bf16),
            pltpu.VMEM((SIDE, RANK, rows), f32),
            pltpu.VMEM((SIDE, RANK, rows), f32),
            pltpu.VMEM((rows, picked), bf16),
            dma,
            dma((TENSOR, 2)),
            dma((4,)),
            dma((QUARTERS, TENSOR)),
            dma((QUARTERS, TENSOR)),
            dma((GROUPS,)),
            dma((GROUPS,)),
            dma((SIDE,)),
            dma((SIDE,)),
            dma((SIDE,)),
            dma((SIDE,)),
            dma((TENSOR,)),
            dma((TENSOR,)),
            dma((TENSOR,)),
            dma((TENSOR,)),
            dma((QUARTERS, TENSOR)),
            dma((QUARTERS, TENSOR)),
        ],
        compiler_params=pltpu.CompilerParams(
            collective_id=0, has_side_effects=True, vmem_limit_bytes=60 * MIB
        ),
    )(
        tokens,
        gate_weight_codes,
        up_weight_codes,
        down_weight_codes,
        gate_channel_scale.reshape(1, -1),
        up_channel_scale.reshape(1, -1),
        down_channel_scale.reshape(1, -1),
        adapter_input_factors,
        adapter_output_factors,
        group_adapter_lists.reshape(-1),
        row_adapter_entry.reshape(1, -1),
        table,
    )


def solution(mesh):
    return jax.shard_map(
        local,
        mesh=mesh,
        in_specs=(
            P("dp", "tensor"),
            P(None, "tensor"),
            P(None, "tensor"),
            P("tensor", None),
            P("tensor"),
            P("tensor"),
            P("tensor"),
            P(None, "dp"),
            P("tensor", "dp"),
            P(),
            P("dp"),
        ),
        out_specs=P("dp", "tensor"),
        check_vma=False,
    )
```

```python
import functools
import math

import jax
import jax.numpy as jnp
import numpy as np
from jax import lax
from jax.experimental import pallas as pl
from jax.experimental.pallas import tpu as pltpu
from jax.sharding import PartitionSpec as P

HIDDEN_UNITS = 14336
RANK = 16
SIDE = 4
TENSOR = SIDE * SIDE
GROUPS = 8
SLOTS = 2
QUARTERS = 4
MIB = 1024 * 1024


def steps(a):
    return min(a, SIDE - a)


def depth(o):
    return steps(o[0]) + steps(o[1])


OFFSETS = sorted(((a, b) for a in range(SIDE) for b in range(SIDE)), key=depth)
LEVELS = [[o for o in OFFSETS if depth(o) == level] for level in range(5)]
ORDER = {o: i for i, o in enumerate(OFFSETS)}


def parent(q, o):
    dz, dy = o
    via = 1 if q % 2 == 0 else SIDE - 1

    def back(a):
        return via if a == 2 else 0

    if q < 2:
        return (dz, back(dy)) if dy else (back(dz), 0)
    return (back(dz), dy) if dz else (0, back(dy))


CHILDREN = {
    (q, o): [c for c in OFFSETS if c != (0, 0) and parent(q, c) == o]
    for q in range(QUARTERS)
    for o in OFFSETS
}


def rotation_table(local_units):
    order = local_units // 28
    index = np.arange(order)
    walsh = np.ones((order, order), np.int64)
    for bit in range(max(order.bit_length() - 1, 0)):
        walsh *= 1 - 2 * ((index[:, None] & index[None, :]) >> bit & 1)
    conference = np.ones((14, 14), np.int64)
    residues = {j * j % 13 for j in range(1, 13)}
    conference[0, 0] = 0
    for i in range(13):
        for j in range(13):
            offset = (j - i) % 13
            conference[i + 1, j + 1] = 0 if offset == 0 else (1 if offset in residues else -1)
    paley = np.kron(conference, np.array([[1, 1], [1, -1]])) + np.kron(
        np.eye(14, dtype=np.int64), np.array([[1, -1], [-1, -1]])
    )
    return np.kron(walsh, paley).astype(np.float32)


def body(
    tokens, wg, wu, wd, gs, us, ds, fa, fb, lists, entry, table, out,
    xs, wv, wdv, tv, acc, hid, gst, ra, rb, rot, rotc, part, rss, rsr,
    fav, fbv, stage, fac, lrz, lry, low,
    own_sem, w_sem, misc_sem, ag_s, ag_r, dp_s, dp_r, lz_s, lz_r, ly_s, ly_r,
    a1_s, a1_r, a2_s, a2_r, rs_s, rs_r,
):
    rows, width = tokens.shape
    units = wg.shape[1]
    quarter = rows // QUARTERS
    panels = units // 128
    share = ra.shape[1]
    d = lax.axis_index("dp")
    t = lax.axis_index("tensor")
    z = lax.div(t, SIDE)
    y = lax.rem(t, SIDE)

    def at(o, sign=1):
        return (
            lax.rem(z + sign * o[0] + SIDE, SIDE) * SIDE + lax.rem(y + sign * o[1] + SIDE, SIDE)
        )

    def remote(src, dst, send, recv, to, axis="tensor"):
        return pltpu.make_async_remote_copy(
            src_ref=src, dst_ref=dst, send_sem=send, recv_sem=recv,
            device_id={axis: to}, device_id_type=pl.DeviceIdType.MESH,
        )

    def send(*args, **kw):
        remote(*args, **kw).start()

    def received(like, semaphore):
        pltpu.make_async_copy(like, like, semaphore).wait()

    barrier = pltpu.get_barrier_semaphore()
    for o in LEVELS[1]:
        pl.semaphore_signal(
            barrier, inc=1, device_id={"tensor": at(o)}, device_id_type=pl.DeviceIdType.MESH
        )
    for i in range(1, GROUPS):
        pl.semaphore_signal(
            barrier, inc=1, device_id={"dp": lax.rem(d + i, GROUPS)},
            device_id_type=pl.DeviceIdType.MESH,
        )

    own = pltpu.make_async_copy(tokens, xs.at[t], own_sem)
    own.start()
    fa_copy = pltpu.make_async_copy(
        fa.at[pl.ds(pl.multiple_of(t * width, width), width), :], fav, misc_sem.at[0]
    )
    fa_copy.start()
    fb_copy = pltpu.make_async_copy(fb, fbv, misc_sem.at[1])
    fb_copy.start()
    for i, o in enumerate(OFFSETS):
        block = pl.ds(pl.multiple_of(at(o, -1) * width, width), width)
        pltpu.make_async_copy(wg.at[block, :], wv.at[i, :, 0:units], w_sem.at[i]).start()
        pltpu.make_async_copy(wu.at[block, :], wv.at[i, :, units : 2 * units], w_sem.at[i]).start()
    table_copy = pltpu.make_async_copy(table, tv, misc_sem.at[2])
    table_copy.start()
    wd_copy = pltpu.make_async_copy(wd, wdv, misc_sem.at[3])
    wd_copy.start()

    fa_copy.wait()
    fb_copy.wait()
    rank_row = lax.broadcasted_iota(jnp.int32, (RANK, GROUPS * RANK), 0)
    column = lax.broadcasted_iota(jnp.int32, (RANK, GROUPS * RANK), 1)
    picks = []
    for g in range(GROUPS):
        for s in range(SLOTS):
            picked = lists[g, s, d]
            picks.append((column == picked * RANK + rank_row).astype(jnp.float32))
    pick = jnp.concatenate(picks, axis=0).astype(jnp.bfloat16)
    nt = (((1,), (1,)), ((), ()))
    stage[:, 0:width] = lax.dot_general(
        pick, fav[...], nt, preferred_element_type=jnp.float32
    ).astype(jnp.bfloat16)
    stage[:, width:] = lax.dot_general(
        pick, fbv[...], nt, preferred_element_type=jnp.float32
    ).astype(jnp.bfloat16)
    block_rows = SLOTS * RANK
    mine = pl.ds(pl.multiple_of(d * block_rows, block_rows), block_rows)
    fac[mine, :] = stage[mine, :]

    pl.semaphore_wait(barrier, len(LEVELS[1]) + GROUPS - 1)

    def rows_of(q):
        return pl.ds(q * quarter, quarter)

    def forward(q, o):
        source = at(o, -1)
        for c in CHILDREN[q, o]:
            hop = (c[0] - o[0], c[1] - o[1])
            src = tokens.at[rows_of(q), :] if o == (0, 0) else xs.at[source, rows_of(q), :]
            send(
                src, xs.at[source, rows_of(q), :],
                ag_s, ag_r.at[q, depth(c)], at(hop),
            )

    def arrived(q, level):
        received(xs.at[0 : len(LEVELS[level]), rows_of(q), :], ag_r.at[q, level])

    def multiply(i, o):
        source = at(o, -1)
        received(wv.at[i], w_sem.at[i])

        @pl.loop(0, 2 * units // 256)
        def _(n):
            columns = pl.ds(pl.multiple_of(n * 256, 256), 256)
            product = jnp.dot(
                xs[source], wv[i, :, columns], preferred_element_type=jnp.float32
            )
            if i == 0:
                acc[:, columns] = product
            else:
                acc[:, columns] += product

    for q in range(QUARTERS):
        forward(q, (0, 0))
    for i in range(1, GROUPS):
        peer = lax.rem(d + i, GROUPS)
        theirs = pl.ds(pl.multiple_of(peer * block_rows, block_rows), block_rows)
        send(stage.at[theirs, :], fac.at[mine, :], dp_s, dp_r, peer, axis="dp")
    own.wait()

    slot_of = lax.broadcasted_iota(jnp.int32, (GROUPS * SLOTS * RANK, rows), 0) // RANK
    chosen = slot_of == entry[...].reshape(1, rows)

    def low_partial():
        received(fac.at[0 : (GROUPS - 1) * block_rows], dp_r)
        everyone = lax.dot_general(
            fac[:, 0:width], xs[t], nt, preferred_element_type=jnp.float32
        )
        kept = jnp.where(chosen, everyone, 0.0)
        lrz[0] = jnp.sum(kept.reshape(GROUPS * SLOTS, RANK, rows), axis=0)
        for i in range(1, SIDE):
            send(lrz.at[0], lrz.at[i], lz_s, lz_r, at((i, 0)))

    def low_along_y():
        received(lrz.at[1:], lz_r)
        lry[0] = (lrz[0] + lrz[1]) + (lrz[2] + lrz[3])
        for i in range(1, SIDE):
            send(lry.at[0], lry.at[i], ly_s, ly_r, at((0, i)))

    def low_whole():
        received(lry.at[1:], ly_r)
        total = (lry[0] + lry[1]) + (lry[2] + lry[3])
        total = total.astype(jnp.bfloat16).astype(jnp.float32)
        spread = jnp.concatenate([total] * (GROUPS * SLOTS), axis=0)
        low[...] = jnp.transpose(jnp.where(chosen, spread, 0.0)).astype(jnp.bfloat16)

    work = [lambda: multiply(0, (0, 0))]
    for level in range(1, 5):
        ready = len(work)
        for q in range(QUARTERS):
            arrived(q, level)
            for o in LEVELS[level]:
                forward(q, o)
            for _ in range(-(-ready // QUARTERS)):
                if ready:
                    work.pop(0)()
                    ready -= 1
        for o in LEVELS[level]:
            work.append(functools.partial(multiply, ORDER[o], o))
        if level < 4:
            work.insert(2, (low_partial, low_along_y, low_whole)[level - 1])
    for item in work:
        item()

    @pl.loop(0, panels)
    def _(j):
        columns = pl.ds(pl.multiple_of(j * 128, 128), 128)
        up_columns = pl.ds(pl.multiple_of(units + j * 128, 128), 128)
        factor_columns = pl.ds(pl.multiple_of(width + j * 128, 128), 128)
        gate = acc[:, columns] * gs[columns].reshape(1, 128)
        extra = jnp.dot(low[...], fac[:, factor_columns], preferred_element_type=jnp.float32)
        up = acc[:, up_columns] * us[columns].reshape(1, 128) + extra
        hid[:, columns] = (gate / (1.0 + jnp.exp(-gate)) * up).astype(jnp.bfloat16)

    table_copy.wait()
    for j in range(0, panels, 2):
        wide = min(2, panels - j)
        turned = jnp.dot(
            hid[...], tv[:, j * 128 : (j + wide) * 128], preferred_element_type=jnp.float32
        ).astype(jnp.bfloat16)
        for k in range(wide):
            gst[(j + k) * rows : (j + k + 1) * rows, :] = turned[:, k * 128 : (k + 1) * 128]
    gst[panels * rows :, :] = jnp.zeros((gst.shape[0] - panels * rows, 128), jnp.bfloat16)

    def share_of(index):
        return pl.ds(pl.multiple_of(index * share, 16), share)

    far_first = OFFSETS[:0:-1]
    for o in far_first:
        peer = at(o)
        send(gst.at[share_of(peer), :], ra.at[t], a1_s, a1_r, peer)
    ra[t] = gst[share_of(t), :]
    received(ra.at[1:], a1_r)
    norm = 1.0 / math.sqrt(HIDDEN_UNITS)

    @pl.loop(0, share // 16)
    def _(k):
        tile = pl.ds(pl.multiple_of(k * 16, 16), 16)
        terms = [ra[i, tile, :].astype(jnp.float32) for i in range(TENSOR)]
        for bit in range(4):
            mixed = list(terms)
            for i in range(TENSOR):
                j = i ^ (1 << bit)
                if i < j:
                    mixed[i] = terms[i] + terms[j]
                    mixed[j] = terms[i] - terms[j]
            terms = mixed
        for i in range(TENSOR):
            rb[i, tile, :] = (terms[i] * norm).astype(jnp.bfloat16)

    for o in far_first:
        peer = at(o)
        send(rb.at[peer], rot.at[share_of(t), :], a2_s, a2_r, peer)
    rot[share_of(t), :] = rb[t]
    received(rot.at[share:, :], a2_r)
    for j in range(panels):
        rotc[:, j * 128 : (j + 1) * 128] = rot[j * rows : (j + 1) * rows, :]

    wd_copy.wait()

    def project(o):
        target = at(o, -1)
        columns = pl.ds(pl.multiple_of(target * width, width), width)
        part[ORDER[o]] = jnp.dot(
            rotc[...], wdv[:, columns], preferred_element_type=jnp.float32
        )

    def collected(q, o):
        total = part[ORDER[o], rows_of(q), :]
        for c in CHILDREN[q, o]:
            total = total + rsr[ORDER[c], rows_of(q), :].astype(jnp.float32)
        return total

    def pass_up(q, o):
        rss[ORDER[o], rows_of(q), :] = collected(q, o).astype(jnp.bfloat16)
        above = parent(q, o)
        hop = (above[0] - o[0], above[1] - o[1])
        send(
            rss.at[ORDER[o], rows_of(q), :], rsr.at[ORDER[o], rows_of(q), :],
            rs_s, rs_r.at[q, depth(o)], at(hop),
        )

    for level in (4, 3, 2, 1):
        for o in LEVELS[level]:
            project(o)
            for q in range(QUARTERS):
                if not CHILDREN[q, o]:
                    pass_up(q, o)
        if level == 1:
            project((0, 0))
        if level < 4:
            for q in range(QUARTERS):
                received(rsr.at[0 : len(LEVELS[level + 1]), rows_of(q), :], rs_r.at[q, level + 1])
                for o in LEVELS[level]:
                    if CHILDREN[q, o]:
                        pass_up(q, o)
    for q in range(QUARTERS):
        received(rsr.at[0 : len(LEVELS[1]), rows_of(q), :], rs_r.at[q, 1])
        out[rows_of(q), :] = (collected(q, (0, 0)) * ds[...].reshape(1, width)).astype(jnp.bfloat16)
    received(xs.at[0 : TENSOR - 1], ag_s)
    received(fac.at[0 : (GROUPS - 1) * block_rows], dp_s)
    received(lrz.at[1:], lz_s)
    received(lry.at[1:], ly_s)
    received(ra.at[1:], a1_s)
    received(ra.at[1:], a2_s)
    received(rss.at[1:], rs_s)


def local(
    tokens,
    gate_weight_codes,
    up_weight_codes,
    down_weight_codes,
    gate_channel_scale,
    up_channel_scale,
    down_channel_scale,
    adapter_input_factors,
    adapter_output_factors,
    group_adapter_lists,
    row_adapter_entry,
):
    rows, width = tokens.shape
    units = gate_weight_codes.shape[1]
    factors = adapter_input_factors.shape[1]
    picked = GROUPS * SLOTS * RANK
    panels = units // 128
    share = -(-panels * rows // (16 * TENSOR)) * 16
    bf16, f32 = jnp.bfloat16, jnp.float32
    table = jnp.asarray(rotation_table(units), bf16)
    hbm = pl.BlockSpec(memory_space=pl.ANY)
    vmem = pl.BlockSpec(memory_space=pltpu.VMEM)
    smem = pl.BlockSpec(memory_space=pltpu.SMEM)
    dma = pltpu.SemaphoreType.DMA
    return pl.pallas_call(
        body,
        out_shape=jax.ShapeDtypeStruct((rows, width), bf16),
        in_specs=[hbm, hbm, hbm, hbm, vmem, vmem, vmem, hbm, hbm, smem, vmem, hbm],
        out_specs=vmem,
        scratch_shapes=[
            pltpu.VMEM((TENSOR, rows, width), bf16),
            pltpu.VMEM((TENSOR, width, 2 * units), bf16),
            pltpu.VMEM(down_weight_codes.shape, bf16),
            pltpu.VMEM((units, units), bf16),
            pltpu.VMEM((rows, 2 * units), f32),
            pltpu.VMEM((rows, units), bf16),
            pltpu.VMEM((TENSOR * share, 128), bf16),
            pltpu.VMEM((TENSOR, share, 128), bf16),
            pltpu.VMEM((TENSOR, share, 128), bf16),
            pltpu.VMEM((TENSOR * share, 128), bf16),
            pltpu.VMEM((rows, units), bf16),
            pltpu.VMEM((TENSOR, rows, width), f32),
            pltpu.VMEM((TENSOR, rows, width), bf16),
            pltpu.VMEM((TENSOR, rows, width), bf16),
            pltpu.VMEM((width, factors), bf16),
            pltpu.VMEM((units, factors), bf16),
            pltpu.VMEM((picked, width + units), bf16),
            pltpu.VMEM((picked, width + units), bf16),
            pltpu.VMEM((SIDE, RANK, rows), f32),
            pltpu.VMEM((SIDE, RANK, rows), f32),
            pltpu.VMEM((rows, picked), bf16),
            dma,
            dma((TENSOR,)),
            dma((4,)),
            dma,
            dma((QUARTERS, 5)),
            dma,
            dma,
            dma,
            dma,
            dma,
            dma,
            dma,
            dma,
            dma,
            dma,
            dma,
            dma((QUARTERS, 5)),
        ],
        compiler_params=pltpu.CompilerParams(
            collective_id=0, has_side_effects=True, vmem_limit_bytes=60 * MIB
        ),
    )(
        tokens,
        gate_weight_codes,
        up_weight_codes,
        down_weight_codes,
        gate_channel_scale,
        up_channel_scale,
        down_channel_scale,
        adapter_input_factors,
        adapter_output_factors,
        jnp.transpose(group_adapter_lists, (0, 2, 1)),
        row_adapter_entry,
        table,
    )


def solution(mesh):
    return jax.shard_map(
        local,
        mesh=mesh,
        in_specs=(
            P("dp", "tensor"),
            P(None, "tensor"),
            P(None, "tensor"),
            P("tensor", None),
            P("tensor"),
            P("tensor"),
            P("tensor"),
            P(None, "dp"),
            P("tensor", "dp"),
            P(),
            P("dp"),
        ),
        out_specs=P("dp", "tensor"),
        check_vma=False,
    )
```

```python
import functools
import math

import jax
import jax.numpy as jnp
import numpy as np
from jax import lax
from jax.experimental import pallas as pl
from jax.experimental.pallas import tpu as pltpu
from jax.sharding import PartitionSpec as P

HIDDEN_UNITS = 14336
RANK = 16
SIDE = 4
TENSOR = SIDE * SIDE
GROUPS = 8
SLOTS = 2
QUARTERS = 4
PARTS = ((0, 208), (208, 176))
TREES = ((0, 2), (1, 3))
TREE_ROWS = {0: (0, 96), 2: (96, 112), 1: (208, 96), 3: (304, 80)}
MIB = 1024 * 1024


def steps(a):
    return min(a, SIDE - a)


def depth(o):
    return steps(o[0]) + steps(o[1])


OFFSETS = sorted(((a, b) for a in range(SIDE) for b in range(SIDE)), key=depth)
ORDER = {o: i for i, o in enumerate(OFFSETS)}
NEAR = [o for o in OFFSETS if depth(o) == 1]
OPPOSITE = [(2, 0), (0, 2)]


def parent(q, o):
    dz, dy = o
    via = 1 if q % 2 == 0 else SIDE - 1
    if q < 2:
        return (dz, via if dy == 2 else 0) if dy else (0, 0)
    return (via if dz == 2 else 0, dy) if dz else (0, 0)


def level_of(q, o):
    return 0 if o == (0, 0) else 1 + level_of(q, parent(q, o))


LEVELS = {
    (q, level): [o for o in OFFSETS if level_of(q, o) == level]
    for q in range(QUARTERS)
    for level in range(5)
}
CHILDREN = {
    (q, o): [c for c in OFFSETS if c != (0, 0) and parent(q, c) == o]
    for q in range(QUARTERS)
    for o in OFFSETS
}
for children in CHILDREN.values():
    children.sort(key=depth, reverse=True)


def share_rows(rows, panels):
    return -(-panels * rows // (16 * TENSOR)) * 16


def rotation_table(local_units):
    order = local_units // 28
    index = np.arange(order)
    walsh = np.ones((order, order), np.int64)
    for bit in range(max(order.bit_length() - 1, 0)):
        walsh *= 1 - 2 * ((index[:, None] & index[None, :]) >> bit & 1)
    conference = np.ones((14, 14), np.int64)
    residues = {j * j % 13 for j in range(1, 13)}
    conference[0, 0] = 0
    for i in range(13):
        for j in range(13):
            offset = (j - i) % 13
            conference[i + 1, j + 1] = 0 if offset == 0 else (1 if offset in residues else -1)
    paley = np.kron(conference, np.array([[1, 1], [1, -1]])) + np.kron(
        np.eye(14, dtype=np.int64), np.array([[1, -1], [-1, -1]])
    )
    return np.kron(walsh, paley).astype(np.float32)


def body(
    tokens, wg, wu, wd, gs, us, ds, fa, fb, lists, entry, table, out,
    xs, wv, wdv, tv, acc, hid, gst, ra, rb, rot, rotc, part, rss, rsr,
    fav, fbv, stage, fac, relay, lrz, lry, low, extra,
    own_sem, w_sem, misc_sem, ag_s, ag_r, dp_s, dp_r, lz_s, lz_r, ly_s, ly_r,
    a1_s, a1_r, a2_s, a2_r, rs_s, rs_r,
):
    rows, width = tokens.shape
    units = wg.shape[1]
    panels = units // 128
    shares = [share_rows(count, panels) for _, count in PARTS]
    bases = [sum(shares[:p]) for p in range(len(PARTS))]
    d = lax.axis_index("dp")
    t = lax.axis_index("tensor")
    z = lax.div(t, SIDE)
    y = lax.rem(t, SIDE)

    def at(o, sign=1):
        return (
            lax.rem(z + sign * o[0] + SIDE, SIDE) * SIDE + lax.rem(y + sign * o[1] + SIDE, SIDE)
        )

    def remote(src, dst, send, recv, to, axis="tensor"):
        return pltpu.make_async_remote_copy(
            src_ref=src, dst_ref=dst, send_sem=send, recv_sem=recv,
            device_id={axis: to}, device_id_type=pl.DeviceIdType.MESH,
        )

    def send(*args, **kw):
        remote(*args, **kw).start()

    def received(like, semaphore):
        pltpu.make_async_copy(like, like, semaphore).wait()

    barrier = pltpu.get_barrier_semaphore()
    for o in NEAR + OPPOSITE:
        pl.semaphore_signal(
            barrier, inc=1, device_id={"tensor": at(o)}, device_id_type=pl.DeviceIdType.MESH
        )
    core = lax.rem(d, 2)
    partner = d + 1 - 2 * core
    along_x = [lax.rem(d + 2 * i, GROUPS) for i in range(1, SIDE)]
    for peer in [partner] + along_x:
        pl.semaphore_signal(
            barrier, inc=1, device_id={"dp": peer}, device_id_type=pl.DeviceIdType.MESH
        )

    own = pltpu.make_async_copy(tokens, xs.at[t], own_sem)
    own.start()
    fa_copy = pltpu.make_async_copy(
        fa.at[pl.ds(pl.multiple_of(t * width, width), width), :], fav, misc_sem.at[0]
    )
    fa_copy.start()
    fb_copy = pltpu.make_async_copy(fb, fbv, misc_sem.at[1])
    fb_copy.start()
    def fetch(first, count):
        for i in range(first, first + count):
            block = pl.ds(pl.multiple_of(at(OFFSETS[i], -1) * width, width), width)
            pltpu.make_async_copy(wg.at[block, :], wv.at[i, :, 0:units], w_sem.at[i]).start()
            pltpu.make_async_copy(
                wu.at[block, :], wv.at[i, :, units : 2 * units], w_sem.at[i]
            ).start()

    fetch(0, 5)
    table_copy = pltpu.make_async_copy(table, tv, misc_sem.at[2])
    wd_copy = pltpu.make_async_copy(wd, wdv, misc_sem.at[3])

    pl.semaphore_wait(barrier, len(NEAR) + len(OPPOSITE) + SIDE)

    def rows_of(q):
        return pl.ds(*TREE_ROWS[q])

    def part_rows(p):
        return pl.ds(*PARTS[p])

    def forward(q, o):
        source = at(o, -1)
        for c in CHILDREN[q, o]:
            hop = (c[0] - o[0], c[1] - o[1])
            src = tokens.at[rows_of(q), :] if o == (0, 0) else xs.at[source, rows_of(q), :]
            send(
                src, xs.at[source, rows_of(q), :],
                ag_s, ag_r.at[q, level_of(q, c)], at(hop),
            )

    def arrived(q, level):
        received(xs.at[0 : len(LEVELS[q, level]), rows_of(q), :], ag_r.at[q, level])

    def load(first, count):
        for i in range(first, first + count):
            received(wv.at[i], w_sem.at[i])

    def multiply(some, first, count):
        sources = [at(OFFSETS[i], -1) for i in range(first, first + count)]
        for n in range(2 * units // 256):
            columns = slice(n * 256, (n + 1) * 256)
            x = jnp.concatenate([xs[source, some, :] for source in sources], axis=1)
            w = wv[first : first + count, :, columns].reshape(count * width, 256)
            product = jnp.dot(x, w, preferred_element_type=jnp.float32)
            if first == 0:
                acc[some, columns] = product
            else:
                acc[some, columns] += product

    for q in TREE_ROWS:
        forward(q, (0, 0))
    fetch(5, 11)

    fa_copy.wait()
    fb_copy.wait()
    rank_row = lax.broadcasted_iota(jnp.int32, (RANK, GROUPS * RANK), 0)
    column = lax.broadcasted_iota(jnp.int32, (RANK, GROUPS * RANK), 1)
    picks = []
    for g in range(GROUPS):
        for s in range(SLOTS):
            picked = lists[g, s, d]
            picks.append((column == picked * RANK + rank_row).astype(jnp.float32))
    pick = jnp.concatenate(picks, axis=0).astype(jnp.bfloat16)
    nt = (((1,), (1,)), ((), ()))
    stage[:, 0:width] = lax.dot_general(
        pick, fav[...], nt, preferred_element_type=jnp.float32
    ).astype(jnp.bfloat16)
    stage[:, width:] = lax.dot_general(
        pick, fbv[...], nt, preferred_element_type=jnp.float32
    ).astype(jnp.bfloat16)
    block_rows = SLOTS * RANK
    mine = pl.ds(pl.multiple_of(d * block_rows, block_rows), block_rows)
    fac[mine, :] = stage[mine, :]

    def block_of(index):
        return pl.ds(pl.multiple_of(index * block_rows, block_rows), block_rows)

    for i in range(SIDE):
        group = lax.rem(partner + 2 * i, GROUPS)
        to = fac.at[mine, :] if i == 0 else relay.at[block_of(i), :]
        send(stage.at[block_of(group), :], to, dp_s, dp_r.at[0], partner, axis="dp")
    for i, peer in enumerate(along_x):
        send(stage.at[block_of(peer), :], fac.at[mine, :], dp_s, dp_r.at[1], peer, axis="dp")

    def relay_factors():
        received(relay.at[...], dp_r.at[0])
        for i, peer in enumerate(along_x):
            send(
                relay.at[block_of(i + 1), :], fac.at[block_of(partner), :],
                dp_s, dp_r.at[1], peer, axis="dp",
            )

    own.wait()

    slot_of = lax.broadcasted_iota(jnp.int32, (GROUPS * SLOTS * RANK, rows), 0) // RANK
    chosen = slot_of == entry[...].reshape(1, rows)

    def low_partial():
        received(fac.at[0 : 2 * (SIDE - 1) * block_rows], dp_r.at[1])
        everyone = lax.dot_general(
            fac[:, 0:width], xs[t], nt, preferred_element_type=jnp.float32
        )
        kept = jnp.where(chosen, everyone, 0.0)
        lrz[0] = jnp.sum(kept.reshape(GROUPS * SLOTS, RANK, rows), axis=0)
        for i in range(1, SIDE):
            send(lrz.at[0], lrz.at[i], lz_s, lz_r, at((i, 0)))

    def low_along_y():
        received(lrz.at[1:], lz_r)
        lry[0] = (lrz[0] + lrz[1]) + (lrz[2] + lrz[3])
        for i in range(1, SIDE):
            send(lry.at[0], lry.at[i], ly_s, ly_r, at((0, i)))

    def low_whole():
        received(lry.at[1:], ly_r)
        total = (lry[0] + lry[1]) + (lry[2] + lry[3])
        total = total.astype(jnp.bfloat16).astype(jnp.float32)
        spread = jnp.concatenate([total] * (GROUPS * SLOTS), axis=0)
        low[...] = jnp.transpose(jnp.where(chosen, spread, 0.0)).astype(jnp.bfloat16)
        for j in range(0, units, 256):
            columns = slice(j, min(j + 256, units))
            factors = fac[:, width + columns.start : width + columns.stop]
            extra[:, columns] = jnp.dot(low[...], factors, preferred_element_type=jnp.float32)

    def step(q, level):
        arrived(q, level)
        for o in LEVELS[q, level]:
            forward(q, o)

    def activate(p):
        some = part_rows(p)

        @pl.loop(0, panels)
        def _(j):
            columns = pl.ds(pl.multiple_of(j * 128, 128), 128)
            up_columns = pl.ds(pl.multiple_of(units + j * 128, 128), 128)
            gate = acc[some, columns] * gs[columns].reshape(1, 128)
            up = acc[some, up_columns] * us[columns].reshape(1, 128) + extra[some, columns]
            hid[some, columns] = (gate / (1.0 + jnp.exp(-gate)) * up).astype(jnp.bfloat16)

    def turn(p):
        count = PARTS[p][1]
        base = TENSOR * bases[p]
        for j in range(0, panels, 2):
            wide = min(2, panels - j)
            turned = jnp.dot(
                hid[part_rows(p), :], tv[:, j * 128 : (j + wide) * 128],
                preferred_element_type=jnp.float32,
            ).astype(jnp.bfloat16)
            for k in range(wide):
                gst[pl.ds(base + (j + k) * count, count), :] = turned[:, k * 128 : (k + 1) * 128]
        rest = TENSOR * shares[p] - panels * count
        if rest:
            gst[pl.ds(base + panels * count, rest), :] = jnp.zeros((rest, 128), jnp.bfloat16)

    def share_of(p, index):
        return pl.ds(pl.multiple_of(TENSOR * bases[p] + index * shares[p], 16), shares[p])

    def slot_of_part(p):
        return pl.ds(bases[p], shares[p])

    far_first = OFFSETS[:0:-1]

    def share_out(p):
        for o in far_first:
            peer = at(o)
            send(
                gst.at[share_of(p, peer), :], ra.at[t, slot_of_part(p), :],
                a1_s, a1_r.at[p], peer,
            )
        ra[t, slot_of_part(p), :] = gst[share_of(p, t), :]

    norm = 1.0 / math.sqrt(HIDDEN_UNITS)

    def mix(p):
        received(ra.at[1:, slot_of_part(p), :], a1_r.at[p])

        @pl.loop(0, shares[p] // 16)
        def _(k):
            tile = pl.ds(pl.multiple_of(bases[p] + k * 16, 16), 16)
            terms = [ra[i, tile, :].astype(jnp.float32) for i in range(TENSOR)]
            for bit in range(4):
                mixed = list(terms)
                for i in range(TENSOR):
                    j = i ^ (1 << bit)
                    if i < j:
                        mixed[i] = terms[i] + terms[j]
                        mixed[j] = terms[i] - terms[j]
                terms = mixed
            for i in range(TENSOR):
                rb[i, tile, :] = (terms[i] * norm).astype(jnp.bfloat16)

        for o in far_first:
            peer = at(o)
            send(
                rb.at[peer, slot_of_part(p), :], rot.at[share_of(p, t), :],
                a2_s, a2_r.at[p], peer,
            )
        rot[share_of(p, t), :] = rb[t, slot_of_part(p), :]

    def gather_back(p):
        received(rot.at[0 : (TENSOR - 1) * shares[p], :], a2_r.at[p])
        count = PARTS[p][1]
        for j in range(panels):
            rotc[part_rows(p), j * 128 : (j + 1) * 128] = rot[
                pl.ds(TENSOR * bases[p] + j * count, count), :
            ]

    def collected(q, o):
        total = part[ORDER[o], rows_of(q), :]
        for c in CHILDREN[q, o]:
            total = total + rsr[ORDER[c], rows_of(q), :].astype(jnp.float32)
        return total

    def pass_up(q, o):
        rss[ORDER[o], rows_of(q), :] = collected(q, o).astype(jnp.bfloat16)
        above = parent(q, o)
        hop = (above[0] - o[0], above[1] - o[1])
        send(
            rss.at[ORDER[o], rows_of(q), :], rsr.at[ORDER[o], rows_of(q), :],
            rs_s, rs_r.at[q, level_of(q, o)], at(hop),
        )

    def project(p):
        some = part_rows(p)
        for o in OFFSETS[::-1]:
            target = at(o, -1)
            columns = pl.ds(pl.multiple_of(target * width, width), width)
            part[ORDER[o], some, :] = jnp.dot(
                rotc[some, :], wdv[:, columns], preferred_element_type=jnp.float32
            )
            for q in TREES[p]:
                if o != (0, 0) and not CHILDREN[q, o]:
                    pass_up(q, o)

    def climb(p, level):
        for q in TREES[p]:
            received(
                rsr.at[0 : len(LEVELS[q, level + 1]), rows_of(q), :], rs_r.at[q, level + 1]
            )
            for o in LEVELS[q, level]:
                if level == 0:
                    total = collected(q, o) * ds[...].reshape(1, width)
                    out[rows_of(q), :] = total.astype(jnp.bfloat16)
                elif CHILDREN[q, o]:
                    pass_up(q, o)

    everything = pl.ds(0, rows)
    load(0, 1)
    multiply(everything, 0, 1)
    step(0, 1)
    relay_factors()
    step(2, 1)
    step(1, 1)
    step(3, 1)
    low_partial()
    load(1, 4)
    multiply(everything, 1, 4)
    step(0, 2)
    step(2, 2)
    low_along_y()
    load(5, 6)
    multiply(part_rows(0), 5, 6)
    step(1, 2)
    step(3, 2)
    table_copy.start()
    wd_copy.start()
    multiply(part_rows(1), 5, 6)
    low_whole()
    load(11, 5)
    step(0, 3)
    step(2, 3)
    multiply(part_rows(0), 11, 5)
    activate(0)
    table_copy.wait()
    turn(0)
    share_out(0)
    step(1, 3)
    step(3, 3)
    multiply(part_rows(1), 11, 5)
    activate(1)
    turn(1)
    share_out(1)
    for p in range(len(PARTS)):
        mix(p)
    wd_copy.wait()
    for p in range(len(PARTS)):
        gather_back(p)
        project(p)
    for level in (2, 1, 0):
        for p in range(len(PARTS)):
            climb(p, level)
    received(xs.at[0 : TENSOR - 1], ag_s)
    received(stage.at[...], dp_s)
    received(fac.at[0 : 2 * block_rows], dp_s)
    received(lrz.at[1:], lz_s)
    received(lry.at[1:], ly_s)
    received(ra.at[1:], a1_s)
    received(ra.at[1:], a2_s)
    received(rss.at[1:], rs_s)


def local(
    tokens,
    gate_weight_codes,
    up_weight_codes,
    down_weight_codes,
    gate_channel_scale,
    up_channel_scale,
    down_channel_scale,
    adapter_input_factors,
    adapter_output_factors,
    group_adapter_lists,
    row_adapter_entry,
):
    rows, width = tokens.shape
    units = gate_weight_codes.shape[1]
    factors = adapter_input_factors.shape[1]
    picked = GROUPS * SLOTS * RANK
    panels = units // 128
    share = sum(share_rows(count, panels) for _, count in PARTS)
    bf16, f32 = jnp.bfloat16, jnp.float32
    table = jnp.asarray(rotation_table(units), bf16)
    hbm = pl.BlockSpec(memory_space=pl.ANY)
    vmem = pl.BlockSpec(memory_space=pltpu.VMEM)
    smem = pl.BlockSpec(memory_space=pltpu.SMEM)
    dma = pltpu.SemaphoreType.DMA
    return pl.pallas_call(
        body,
        out_shape=pltpu.VMEM((rows, width), bf16),
        in_specs=[hbm, hbm, hbm, hbm, vmem, vmem, vmem, hbm, hbm, smem, vmem, hbm],
        out_specs=vmem,
        scratch_shapes=[
            pltpu.VMEM((TENSOR, rows, width), bf16),
            pltpu.VMEM((TENSOR, width, 2 * units), bf16),
            pltpu.VMEM(down_weight_codes.shape, bf16),
            pltpu.VMEM((units, units), bf16),
            pltpu.VMEM((rows, 2 * units), f32),
            pltpu.VMEM((rows, units), bf16),
            pltpu.VMEM((TENSOR * share, 128), bf16),
            pltpu.VMEM((TENSOR, share, 128), bf16),
            pltpu.VMEM((TENSOR, share, 128), bf16),
            pltpu.VMEM((TENSOR * share, 128), bf16),
            pltpu.VMEM((rows, units), bf16),
            pltpu.VMEM((TENSOR, rows, width), f32),
            pltpu.VMEM((TENSOR, rows, width), bf16),
            pltpu.VMEM((TENSOR, rows, width), bf16),
            pltpu.VMEM((width, factors), bf16),
            pltpu.VMEM((units, factors), bf16),
            pltpu.VMEM((picked, width + units), bf16),
            pltpu.VMEM((picked, width + units), bf16),
            pltpu.VMEM((SIDE * SLOTS * RANK, width + units), bf16),
            pltpu.VMEM((SIDE, RANK, rows), f32),
            pltpu.VMEM((SIDE, RANK, rows), f32),
            pltpu.VMEM((rows, picked), bf16),
            pltpu.VMEM((rows, units), f32),
            dma,
            dma((TENSOR,)),
            dma((4,)),
            dma,
            dma((QUARTERS, SIDE)),
            dma,
            dma((2,)),
            dma,
            dma,
            dma,
            dma,
            dma,
            dma((len(PARTS),)),
            dma,
            dma((len(PARTS),)),
            dma,
            dma((QUARTERS, SIDE)),
        ],
        compiler_params=pltpu.CompilerParams(
            collective_id=0, has_side_effects=True, vmem_limit_bytes=60 * MIB
        ),
    )(
        tokens,
        gate_weight_codes,
        up_weight_codes,
        down_weight_codes,
        gate_channel_scale,
        up_channel_scale,
        down_channel_scale,
        adapter_input_factors,
        adapter_output_factors,
        jnp.transpose(group_adapter_lists, (0, 2, 1)),
        row_adapter_entry,
        table,
    )


def solution(mesh):
    return jax.shard_map(
        local,
        mesh=mesh,
        in_specs=(
            P("dp", "tensor"),
            P(None, "tensor"),
            P(None, "tensor"),
            P("tensor", None),
            P("tensor"),
            P("tensor"),
            P("tensor"),
            P(None, "dp"),
            P("tensor", "dp"),
            P(),
            P("dp"),
        ),
        out_specs=P("dp", "tensor"),
        check_vma=False,
    )
```

```python
import functools
import math

import jax
import jax.numpy as jnp
import numpy as np
from jax import lax
from jax.experimental import pallas as pl
from jax.experimental.pallas import tpu as pltpu
from jax.sharding import PartitionSpec as P

HIDDEN_UNITS = 14336
RANK = 16
SIDE = 4
TENSOR = SIDE * SIDE
GROUPS = 8
SLOTS = 2
QUARTERS = 4
PARTS = ((0, 208), (208, 176))
TREES = ((0, 2), (1, 3))
TREE_ROWS = {0: (0, 96), 2: (96, 112), 1: (208, 96), 3: (304, 80)}
MIB = 1024 * 1024


def steps(a):
    return min(a, SIDE - a)


def depth(o):
    return steps(o[0]) + steps(o[1])


OFFSETS = sorted(((a, b) for a in range(SIDE) for b in range(SIDE)), key=depth)
ORDER = {o: i for i, o in enumerate(OFFSETS)}
NEAR = [o for o in OFFSETS if depth(o) == 1]
OPPOSITE = [(2, 0), (0, 2)]


def parent(q, o):
    dz, dy = o
    via = 1 if q % 2 == 0 else SIDE - 1
    if q < 2:
        return (dz, via if dy == 2 else 0) if dy else (0, 0)
    return (via if dz == 2 else 0, dy) if dz else (0, 0)


def level_of(q, o):
    return 0 if o == (0, 0) else 1 + level_of(q, parent(q, o))


LEVELS = {
    (q, level): [o for o in OFFSETS if level_of(q, o) == level]
    for q in range(QUARTERS)
    for level in range(5)
}
CHILDREN = {
    (q, o): [c for c in OFFSETS if c != (0, 0) and parent(q, c) == o]
    for q in range(QUARTERS)
    for o in OFFSETS
}
for children in CHILDREN.values():
    children.sort(key=depth, reverse=True)


def share_rows(rows, panels):
    return -(-panels * rows // (16 * TENSOR)) * 16


def rotation_table(local_units):
    order = local_units // 28
    index = np.arange(order)
    walsh = np.ones((order, order), np.int64)
    for bit in range(max(order.bit_length() - 1, 0)):
        walsh *= 1 - 2 * ((index[:, None] & index[None, :]) >> bit & 1)
    conference = np.ones((14, 14), np.int64)
    residues = {j * j % 13 for j in range(1, 13)}
    conference[0, 0] = 0
    for i in range(13):
        for j in range(13):
            offset = (j - i) % 13
            conference[i + 1, j + 1] = 0 if offset == 0 else (1 if offset in residues else -1)
    paley = np.kron(conference, np.array([[1, 1], [1, -1]])) + np.kron(
        np.eye(14, dtype=np.int64), np.array([[1, -1], [-1, -1]])
    )
    return np.kron(walsh, paley).astype(np.float32)


def body(
    tokens, wg, wu, wd, gs, us, ds, fa, fb, lists, entry, table, out,
    xs, wv, wdv, tv, acc, hid, gst, ra, rb, rot, rotc, part, rss, rsr,
    fav, fbv, stage, fac, lrz, lry, low, extra,
    own_sem, w_sem, misc_sem, ag_s, ag_r, dp_s, dp_r, lz_s, lz_r, ly_s, ly_r,
    a1_s, a1_r, a2_s, a2_r, rs_s, rs_r,
):
    rows, width = tokens.shape
    units = wg.shape[1]
    panels = units // 128
    shares = [share_rows(count, panels) for _, count in PARTS]
    bases = [sum(shares[:p]) for p in range(len(PARTS))]
    d = lax.axis_index("dp")
    t = lax.axis_index("tensor")
    z = lax.div(t, SIDE)
    y = lax.rem(t, SIDE)

    def at(o, sign=1):
        return (
            lax.rem(z + sign * o[0] + SIDE, SIDE) * SIDE + lax.rem(y + sign * o[1] + SIDE, SIDE)
        )

    def remote(src, dst, send, recv, to, axis="tensor"):
        return pltpu.make_async_remote_copy(
            src_ref=src, dst_ref=dst, send_sem=send, recv_sem=recv,
            device_id={axis: to}, device_id_type=pl.DeviceIdType.MESH,
        )

    def send(*args, **kw):
        remote(*args, **kw).start()

    def received(like, semaphore):
        pltpu.make_async_copy(like, like, semaphore).wait()

    barrier = pltpu.get_barrier_semaphore()
    for o in NEAR + OPPOSITE:
        pl.semaphore_signal(
            barrier, inc=1, device_id={"tensor": at(o)}, device_id_type=pl.DeviceIdType.MESH
        )
    others = [lax.rem(d + i, GROUPS) for i in range(1, GROUPS)]
    for peer in others:
        pl.semaphore_signal(
            barrier, inc=1, device_id={"dp": peer}, device_id_type=pl.DeviceIdType.MESH
        )

    own = pltpu.make_async_copy(tokens, xs.at[t], own_sem)
    own.start()
    fa_copy = pltpu.make_async_copy(
        fa.at[pl.ds(pl.multiple_of(t * width, width), width), :], fav, misc_sem.at[0]
    )
    fa_copy.start()
    fb_copy = pltpu.make_async_copy(fb, fbv, misc_sem.at[1])
    fb_copy.start()
    def fetch(first, count):
        for i in range(first, first + count):
            block = pl.ds(pl.multiple_of(at(OFFSETS[i], -1) * width, width), width)
            pltpu.make_async_copy(wg.at[block, :], wv.at[i, :, 0:units], w_sem.at[i]).start()
            pltpu.make_async_copy(
                wu.at[block, :], wv.at[i, :, units : 2 * units], w_sem.at[i]
            ).start()

    fetch(0, 5)
    table_copy = pltpu.make_async_copy(table, tv, misc_sem.at[2])
    wd_copy = pltpu.make_async_copy(wd, wdv, misc_sem.at[3])

    fa_copy.wait()
    fb_copy.wait()
    rank_row = lax.broadcasted_iota(jnp.int32, (RANK, GROUPS * RANK), 0)
    column = lax.broadcasted_iota(jnp.int32, (RANK, GROUPS * RANK), 1)
    picks = []
    for g in range(GROUPS):
        for s in range(SLOTS):
            picked = lists[g, s, d]
            picks.append((column == picked * RANK + rank_row).astype(jnp.float32))
    pick = jnp.concatenate(picks, axis=0).astype(jnp.bfloat16)
    nt = (((1,), (1,)), ((), ()))
    stage[:, 0:width] = lax.dot_general(
        pick, fav[...], nt, preferred_element_type=jnp.float32
    ).astype(jnp.bfloat16)
    stage[:, width:] = lax.dot_general(
        pick, fbv[...], nt, preferred_element_type=jnp.float32
    ).astype(jnp.bfloat16)
    block_rows = SLOTS * RANK
    mine = pl.ds(pl.multiple_of(d * block_rows, block_rows), block_rows)
    fac[mine, :] = stage[mine, :]

    pl.semaphore_wait(barrier, len(NEAR) + len(OPPOSITE) + GROUPS - 1)

    def rows_of(q):
        return pl.ds(*TREE_ROWS[q])

    def part_rows(p):
        return pl.ds(*PARTS[p])

    def forward(q, o):
        source = at(o, -1)
        for c in CHILDREN[q, o]:
            hop = (c[0] - o[0], c[1] - o[1])
            src = tokens.at[rows_of(q), :] if o == (0, 0) else xs.at[source, rows_of(q), :]
            send(
                src, xs.at[source, rows_of(q), :],
                ag_s, ag_r.at[q, level_of(q, c)], at(hop),
            )

    def arrived(q, level):
        received(xs.at[0 : len(LEVELS[q, level]), rows_of(q), :], ag_r.at[q, level])

    def load(first, count):
        for i in range(first, first + count):
            received(wv.at[i], w_sem.at[i])

    def multiply(some, first, count):
        sources = [at(OFFSETS[i], -1) for i in range(first, first + count)]
        for n in range(2 * units // 256):
            columns = slice(n * 256, (n + 1) * 256)
            x = jnp.concatenate([xs[source, some, :] for source in sources], axis=1)
            w = wv[first : first + count, :, columns].reshape(count * width, 256)
            product = jnp.dot(x, w, preferred_element_type=jnp.float32)
            if first == 0:
                acc[some, columns] = product
            else:
                acc[some, columns] += product

    def block_of(index):
        return pl.ds(pl.multiple_of(index * block_rows, block_rows), block_rows)

    into, out_of = slice(0, width), slice(width, width + units)
    for peer in others:
        send(
            stage.at[block_of(peer), into], fac.at[mine, into], dp_s, dp_r.at[0], peer, axis="dp"
        )
    for q in TREE_ROWS:
        forward(q, (0, 0))
    for peer in others:
        send(
            stage.at[block_of(peer), out_of], fac.at[mine, out_of],
            dp_s, dp_r.at[1], peer, axis="dp",
        )
    fetch(5, 11)

    own.wait()

    slot_of = lax.broadcasted_iota(jnp.int32, (GROUPS * SLOTS * RANK, rows), 0) // RANK
    chosen = slot_of == entry[...].reshape(1, rows)

    def low_partial():
        received(fac.at[0 : (GROUPS - 1) * block_rows, into], dp_r.at[0])
        everyone = lax.dot_general(
            fac[:, 0:width], xs[t], nt, preferred_element_type=jnp.float32
        )
        kept = jnp.where(chosen, everyone, 0.0)
        lrz[0] = jnp.sum(kept.reshape(GROUPS * SLOTS, RANK, rows), axis=0)
        for i in range(1, SIDE):
            send(lrz.at[0], lrz.at[i], lz_s, lz_r, at((i, 0)))

    def low_along_y():
        received(lrz.at[1:], lz_r)
        lry[0] = (lrz[0] + lrz[1]) + (lrz[2] + lrz[3])
        for i in range(1, SIDE):
            send(lry.at[0], lry.at[i], ly_s, ly_r, at((0, i)))

    def low_whole():
        received(lry.at[1:], ly_r)
        received(fac.at[0 : (GROUPS - 1) * block_rows, out_of], dp_r.at[1])
        total = (lry[0] + lry[1]) + (lry[2] + lry[3])
        total = total.astype(jnp.bfloat16).astype(jnp.float32)
        spread = jnp.concatenate([total] * (GROUPS * SLOTS), axis=0)
        low[...] = jnp.transpose(jnp.where(chosen, spread, 0.0)).astype(jnp.bfloat16)
        for j in range(0, units, 256):
            columns = slice(j, min(j + 256, units))
            factors = fac[:, width + columns.start : width + columns.stop]
            extra[:, columns] = jnp.dot(low[...], factors, preferred_element_type=jnp.float32)

    def step(q, level):
        arrived(q, level)
        for o in LEVELS[q, level]:
            forward(q, o)

    def activate(p):
        some = part_rows(p)

        @pl.loop(0, panels)
        def _(j):
            columns = pl.ds(pl.multiple_of(j * 128, 128), 128)
            up_columns = pl.ds(pl.multiple_of(units + j * 128, 128), 128)
            gate = acc[some, columns] * gs[columns].reshape(1, 128)
            up = acc[some, up_columns] * us[columns].reshape(1, 128) + extra[some, columns]
            hid[some, columns] = (gate / (1.0 + jnp.exp(-gate)) * up).astype(jnp.bfloat16)

    def turn(p):
        count = PARTS[p][1]
        base = TENSOR * bases[p]
        for j in range(0, panels, 2):
            wide = min(2, panels - j)
            turned = jnp.dot(
                hid[part_rows(p), :], tv[:, j * 128 : (j + wide) * 128],
                preferred_element_type=jnp.float32,
            ).astype(jnp.bfloat16)
            for k in range(wide):
                gst[pl.ds(base + (j + k) * count, count), :] = turned[:, k * 128 : (k + 1) * 128]
        rest = TENSOR * shares[p] - panels * count
        if rest:
            gst[pl.ds(base + panels * count, rest), :] = jnp.zeros((rest, 128), jnp.bfloat16)

    def share_of(p, index):
        return pl.ds(pl.multiple_of(TENSOR * bases[p] + index * shares[p], 16), shares[p])

    def slot_of_part(p):
        return pl.ds(bases[p], shares[p])

    far_first = OFFSETS[:0:-1]

    def share_out(p):
        for o in far_first:
            peer = at(o)
            send(
                gst.at[share_of(p, peer), :], ra.at[t, slot_of_part(p), :],
                a1_s, a1_r.at[p], peer,
            )
        ra[t, slot_of_part(p), :] = gst[share_of(p, t), :]

    norm = 1.0 / math.sqrt(HIDDEN_UNITS)

    def mix(p):
        received(ra.at[1:, slot_of_part(p), :], a1_r.at[p])

        @pl.loop(0, shares[p] // 16)
        def _(k):
            tile = pl.ds(pl.multiple_of(bases[p] + k * 16, 16), 16)
            terms = [ra[i, tile, :].astype(jnp.float32) for i in range(TENSOR)]
            for bit in range(4):
                mixed = list(terms)
                for i in range(TENSOR):
                    j = i ^ (1 << bit)
                    if i < j:
                        mixed[i] = terms[i] + terms[j]
                        mixed[j] = terms[i] - terms[j]
                terms = mixed
            for i in range(TENSOR):
                rb[i, tile, :] = (terms[i] * norm).astype(jnp.bfloat16)

        for o in far_first:
            peer = at(o)
            send(
                rb.at[peer, slot_of_part(p), :], rot.at[share_of(p, t), :],
                a2_s, a2_r.at[p], peer,
            )
        rot[share_of(p, t), :] = rb[t, slot_of_part(p), :]

    def gather_back(p):
        received(rot.at[0 : (TENSOR - 1) * shares[p], :], a2_r.at[p])
        count = PARTS[p][1]
        for j in range(panels):
            rotc[part_rows(p), j * 128 : (j + 1) * 128] = rot[
                pl.ds(TENSOR * bases[p] + j * count, count), :
            ]

    def collected(q, o):
        total = part[ORDER[o], rows_of(q), :]
        for c in CHILDREN[q, o]:
            total = total + rsr[ORDER[c], rows_of(q), :].astype(jnp.float32)
        return total

    def pass_up(q, o):
        rss[ORDER[o], rows_of(q), :] = collected(q, o).astype(jnp.bfloat16)
        above = parent(q, o)
        hop = (above[0] - o[0], above[1] - o[1])
        send(
            rss.at[ORDER[o], rows_of(q), :], rsr.at[ORDER[o], rows_of(q), :],
            rs_s, rs_r.at[q, level_of(q, o)], at(hop),
        )

    def project(p, offsets):
        some = part_rows(p)
        for o in offsets:
            target = at(o, -1)
            columns = pl.ds(pl.multiple_of(target * width, width), width)
            part[ORDER[o], some, :] = jnp.dot(
                rotc[some, :], wdv[:, columns], preferred_element_type=jnp.float32
            )
            for q in TREES[p]:
                if o != (0, 0) and not CHILDREN[q, o]:
                    pass_up(q, o)

    def climb(p, level):
        for q in TREES[p]:
            received(
                rsr.at[0 : len(LEVELS[q, level + 1]), rows_of(q), :], rs_r.at[q, level + 1]
            )
            for o in LEVELS[q, level]:
                if level == 0:
                    total = collected(q, o) * ds[...].reshape(1, width)
                    out[rows_of(q), :] = total.astype(jnp.bfloat16)
                elif CHILDREN[q, o]:
                    pass_up(q, o)

    everything = pl.ds(0, rows)
    load(0, 1)
    multiply(everything, 0, 1)
    low_partial()
    step(0, 1)
    step(2, 1)
    low_along_y()
    step(1, 1)
    step(3, 1)
    load(1, 4)
    multiply(everything, 1, 4)
    step(0, 2)
    step(2, 2)
    step(1, 2)
    step(3, 2)
    load(5, 6)
    multiply(part_rows(0), 5, 6)
    low_whole()
    table_copy.start()
    wd_copy.start()
    multiply(part_rows(1), 5, 6)
    load(11, 5)
    step(0, 3)
    step(2, 3)
    multiply(part_rows(0), 11, 5)
    activate(0)
    table_copy.wait()
    turn(0)
    share_out(0)
    step(1, 3)
    step(3, 3)
    multiply(part_rows(1), 11, 5)
    activate(1)
    turn(1)
    share_out(1)
    for p in range(len(PARTS)):
        mix(p)
    wd_copy.wait()
    gather_back(0)
    project(0, OFFSETS[::-1])
    gather_back(1)
    project(1, OFFSETS[::-1])
    for level in (2, 1, 0):
        for p in range(len(PARTS)):
            climb(p, level)
    received(xs.at[0 : TENSOR - 1], ag_s)
    received(fac.at[0 : (GROUPS - 1) * block_rows], dp_s)
    received(lrz.at[1:], lz_s)
    received(lry.at[1:], ly_s)
    received(ra.at[1:], a1_s)
    received(ra.at[1:], a2_s)
    received(rss.at[1:], rs_s)


def local(
    tokens,
    gate_weight_codes,
    up_weight_codes,
    down_weight_codes,
    gate_channel_scale,
    up_channel_scale,
    down_channel_scale,
    adapter_input_factors,
    adapter_output_factors,
    group_adapter_lists,
    row_adapter_entry,
):
    rows, width = tokens.shape
    units = gate_weight_codes.shape[1]
    factors = adapter_input_factors.shape[1]
    picked = GROUPS * SLOTS * RANK
    panels = units // 128
    share = sum(share_rows(count, panels) for _, count in PARTS)
    bf16, f32 = jnp.bfloat16, jnp.float32
    table = jnp.asarray(rotation_table(units), bf16)
    hbm = pl.BlockSpec(memory_space=pl.ANY)
    vmem = pl.BlockSpec(memory_space=pltpu.VMEM)
    smem = pl.BlockSpec(memory_space=pltpu.SMEM)
    dma = pltpu.SemaphoreType.DMA
    return pl.pallas_call(
        body,
        out_shape=pltpu.VMEM((rows, width), bf16),
        in_specs=[hbm, hbm, hbm, hbm, vmem, vmem, vmem, hbm, hbm, smem, vmem, hbm],
        out_specs=vmem,
        scratch_shapes=[
            pltpu.VMEM((TENSOR, rows, width), bf16),
            pltpu.VMEM((TENSOR, width, 2 * units), bf16),
            pltpu.VMEM(down_weight_codes.shape, bf16),
            pltpu.VMEM((units, units), bf16),
            pltpu.VMEM((rows, 2 * units), f32),
            pltpu.VMEM((rows, units), bf16),
            pltpu.VMEM((TENSOR * share, 128), bf16),
            pltpu.VMEM((TENSOR, share, 128), bf16),
            pltpu.VMEM((TENSOR, share, 128), bf16),
            pltpu.VMEM((TENSOR * share, 128), bf16),
            pltpu.VMEM((rows, units), bf16),
            pltpu.VMEM((TENSOR, rows, width), f32),
            pltpu.VMEM((TENSOR, rows, width), bf16),
            pltpu.VMEM((TENSOR, rows, width), bf16),
            pltpu.VMEM((width, factors), bf16),
            pltpu.VMEM((units, factors), bf16),
            pltpu.VMEM((picked, width + units), bf16),
            pltpu.VMEM((picked, width + units), bf16),
            pltpu.VMEM((SIDE, RANK, rows), f32),
            pltpu.VMEM((SIDE, RANK, rows), f32),
            pltpu.VMEM((rows, picked), bf16),
            pltpu.VMEM((rows, units), f32),
            dma,
            dma((TENSOR,)),
            dma((4,)),
            dma,
            dma((QUARTERS, SIDE)),
            dma,
            dma((2,)),
            dma,
            dma,
            dma,
            dma,
            dma,
            dma((len(PARTS),)),
            dma,
            dma((len(PARTS),)),
            dma,
            dma((QUARTERS, SIDE)),
        ],
        compiler_params=pltpu.CompilerParams(
            collective_id=0, has_side_effects=True, vmem_limit_bytes=60 * MIB
        ),
    )(
        tokens,
        gate_weight_codes,
        up_weight_codes,
        down_weight_codes,
        gate_channel_scale,
        up_channel_scale,
        down_channel_scale,
        adapter_input_factors,
        adapter_output_factors,
        jnp.transpose(group_adapter_lists, (0, 2, 1)),
        row_adapter_entry,
        table,
    )


def solution(mesh):
    return jax.shard_map(
        local,
        mesh=mesh,
        in_specs=(
            P("dp", "tensor"),
            P(None, "tensor"),
            P(None, "tensor"),
            P("tensor", None),
            P("tensor"),
            P("tensor"),
            P("tensor"),
            P(None, "dp"),
            P("tensor", "dp"),
            P(),
            P("dp"),
        ),
        out_specs=P("dp", "tensor"),
        check_vma=False,
    )
```

```python
import functools
import math

import jax
import jax.numpy as jnp
import numpy as np
from jax import lax
from jax.experimental import pallas as pl
from jax.experimental.pallas import tpu as pltpu
from jax.sharding import PartitionSpec as P

HIDDEN_UNITS = 14336
RANK = 16
SIDE = 4
TENSOR = SIDE * SIDE
GROUPS = 8
SLOTS = 2
QUARTERS = 4
PARTS = ((0, 208), (208, 176))
TREES = ((0, 2), (1, 3))
TREE_ROWS = {0: (0, 96), 2: (96, 112), 1: (208, 96), 3: (304, 80)}
GROUPS_OF_BLOCKS = ((0, 1), (1, 4), (5, 6), (11, 5))
MIB = 1024 * 1024


def steps(a):
    return min(a, SIDE - a)


def depth(o):
    return steps(o[0]) + steps(o[1])


OFFSETS = sorted(((a, b) for a in range(SIDE) for b in range(SIDE)), key=depth)
ORDER = {o: i for i, o in enumerate(OFFSETS)}
NEAR = [o for o in OFFSETS if depth(o) == 1]
OPPOSITE = [(2, 0), (0, 2)]


def parent(q, o):
    dz, dy = o
    via = 1 if q % 2 == 0 else SIDE - 1
    if q < 2:
        return (dz, via if dy == 2 else 0) if dy else (0, 0)
    return (via if dz == 2 else 0, dy) if dz else (0, 0)


def level_of(q, o):
    return 0 if o == (0, 0) else 1 + level_of(q, parent(q, o))


LEVELS = {
    (q, level): [o for o in OFFSETS if level_of(q, o) == level]
    for q in range(QUARTERS)
    for level in range(5)
}
CHILDREN = {
    (q, o): [c for c in OFFSETS if c != (0, 0) and parent(q, c) == o]
    for q in range(QUARTERS)
    for o in OFFSETS
}
for children in CHILDREN.values():
    children.sort(key=depth, reverse=True)


def share_rows(rows, panels):
    return -(-panels * rows // (16 * TENSOR)) * 16


def rotation_table(local_units):
    order = local_units // 28
    index = np.arange(order)
    walsh = np.ones((order, order), np.int64)
    for bit in range(max(order.bit_length() - 1, 0)):
        walsh *= 1 - 2 * ((index[:, None] & index[None, :]) >> bit & 1)
    conference = np.ones((14, 14), np.int64)
    residues = {j * j % 13 for j in range(1, 13)}
    conference[0, 0] = 0
    for i in range(13):
        for j in range(13):
            offset = (j - i) % 13
            conference[i + 1, j + 1] = 0 if offset == 0 else (1 if offset in residues else -1)
    paley = np.kron(conference, np.array([[1, 1], [1, -1]])) + np.kron(
        np.eye(14, dtype=np.int64), np.array([[1, -1], [-1, -1]])
    )
    return np.kron(walsh, paley).astype(np.float32)


def body(
    tokens, wg, wu, wd, gs_in, us_in, ds_in, fa, fb, lists_in, entry_in, table, out,
    xs, wv, wdv, tv, acc, hid, gst, ra, rb, rot, rotc, part, rss, rsr,
    fav, fbv, stage, fac, lrz, lry, low, extra, gs, us, ds, lists, entry,
    own_sem, w_sem, misc_sem, ag_s, ag_r, dp_s, dp_r, lz_s, lz_r, ly_s, ly_r,
    a1_s, a1_r, a2_s, a2_r, rs_s, rs_r,
):
    rows, width = tokens.shape
    units = wg.shape[1]
    panels = units // 128
    shares = [share_rows(count, panels) for _, count in PARTS]
    bases = [sum(shares[:p]) for p in range(len(PARTS))]
    d = lax.axis_index("dp")
    t = lax.axis_index("tensor")
    z = lax.div(t, SIDE)
    y = lax.rem(t, SIDE)

    def at(o, sign=1):
        return (
            lax.rem(z + sign * o[0] + SIDE, SIDE) * SIDE + lax.rem(y + sign * o[1] + SIDE, SIDE)
        )

    def remote(src, dst, send, recv, to, axis="tensor"):
        return pltpu.make_async_remote_copy(
            src_ref=src, dst_ref=dst, send_sem=send, recv_sem=recv,
            device_id={axis: to}, device_id_type=pl.DeviceIdType.MESH,
        )

    def send(*args, **kw):
        remote(*args, **kw).start()

    def received(like, semaphore):
        pltpu.make_async_copy(like, like, semaphore).wait()

    barrier = pltpu.get_barrier_semaphore()
    for o in NEAR + OPPOSITE:
        pl.semaphore_signal(
            barrier, inc=1, device_id={"tensor": at(o)}, device_id_type=pl.DeviceIdType.MESH
        )
    others = [lax.rem(d + i, GROUPS) for i in range(1, GROUPS)]
    for peer in others:
        pl.semaphore_signal(
            barrier, inc=1, device_id={"dp": peer}, device_id_type=pl.DeviceIdType.MESH
        )

    small = [
        pltpu.make_async_copy(src, dst, misc_sem.at[4 + i])
        for i, (src, dst) in enumerate(
            ((lists_in, lists), (entry_in, entry), (gs_in, gs), (us_in, us), (ds_in, ds))
        )
    ]
    small[0].start()
    own = pltpu.make_async_copy(tokens, xs.at[t], own_sem)
    own.start()
    fa_copy = pltpu.make_async_copy(
        fa.at[pl.ds(pl.multiple_of(t * width, width), width), :], fav, misc_sem.at[0]
    )
    fa_copy.start()
    fb_copy = pltpu.make_async_copy(fb, fbv, misc_sem.at[1])
    fb_copy.start()
    for copy in small[1:]:
        copy.start()
    def fetch(group):
        first, count = GROUPS_OF_BLOCKS[group]
        for i in range(first, first + count):
            block = pl.ds(pl.multiple_of(at(OFFSETS[i], -1) * width, width), width)
            pltpu.make_async_copy(wg.at[block, :], wv.at[i, :, 0:units], w_sem.at[group]).start()
            pltpu.make_async_copy(
                wu.at[block, :], wv.at[i, :, units : 2 * units], w_sem.at[group]
            ).start()

    fetch(0)
    fetch(1)
    table_copy = pltpu.make_async_copy(table, tv, misc_sem.at[2])
    wd_copy = pltpu.make_async_copy(wd, wdv, misc_sem.at[3])

    small[0].wait()
    fa_copy.wait()
    fb_copy.wait()
    rank_row = lax.broadcasted_iota(jnp.int32, (RANK, GROUPS * RANK), 0)
    column = lax.broadcasted_iota(jnp.int32, (RANK, GROUPS * RANK), 1)
    picks = []
    for g in range(GROUPS):
        for s in range(SLOTS):
            picked = lists[g, s, d]
            picks.append((column == picked * RANK + rank_row).astype(jnp.float32))
    pick = jnp.concatenate(picks, axis=0).astype(jnp.bfloat16)
    nt = (((1,), (1,)), ((), ()))
    stage[:, 0:width] = lax.dot_general(
        pick, fav[...], nt, preferred_element_type=jnp.float32
    ).astype(jnp.bfloat16)
    stage[:, width:] = lax.dot_general(
        pick, fbv[...], nt, preferred_element_type=jnp.float32
    ).astype(jnp.bfloat16)
    block_rows = SLOTS * RANK
    mine = pl.ds(pl.multiple_of(d * block_rows, block_rows), block_rows)
    fac[mine, :] = stage[mine, :]

    pl.semaphore_wait(barrier, len(NEAR) + len(OPPOSITE) + GROUPS - 1)

    def rows_of(q):
        return pl.ds(*TREE_ROWS[q])

    def part_rows(p):
        return pl.ds(*PARTS[p])

    def forward(q, o):
        source = at(o, -1)
        for c in CHILDREN[q, o]:
            hop = (c[0] - o[0], c[1] - o[1])
            src = tokens.at[rows_of(q), :] if o == (0, 0) else xs.at[source, rows_of(q), :]
            send(
                src, xs.at[source, rows_of(q), :],
                ag_s, ag_r.at[q, level_of(q, c)], at(hop),
            )

    def arrived(q, level):
        received(xs.at[0 : len(LEVELS[q, level]), rows_of(q), :], ag_r.at[q, level])

    def load(group):
        first, count = GROUPS_OF_BLOCKS[group]
        received(wv.at[first : first + count], w_sem.at[group])

    def multiply(some, first, count):
        sources = [at(OFFSETS[i], -1) for i in range(first, first + count)]
        for n in range(2 * units // 256):
            columns = slice(n * 256, (n + 1) * 256)
            x = jnp.concatenate([xs[source, some, :] for source in sources], axis=1)
            w = wv[first : first + count, :, columns].reshape(count * width, 256)
            product = jnp.dot(x, w, preferred_element_type=jnp.float32)
            if first == 0:
                acc[some, columns] = product
            else:
                acc[some, columns] += product

    def block_of(index):
        return pl.ds(pl.multiple_of(index * block_rows, block_rows), block_rows)

    into, out_of = slice(0, width), slice(width, width + units)
    for peer in others:
        send(
            stage.at[block_of(peer), into], fac.at[mine, into], dp_s, dp_r.at[0], peer, axis="dp"
        )
    for q in TREE_ROWS:
        forward(q, (0, 0))
    for peer in others:
        send(
            stage.at[block_of(peer), out_of], fac.at[mine, out_of],
            dp_s, dp_r.at[1], peer, axis="dp",
        )
    fetch(2)
    fetch(3)

    own.wait()
    for copy in small[1:]:
        copy.wait()

    slot_of = lax.broadcasted_iota(jnp.int32, (GROUPS * SLOTS * RANK, rows), 0) // RANK
    chosen = slot_of == entry[...].reshape(1, rows)

    def low_partial():
        received(fac.at[0 : (GROUPS - 1) * block_rows, into], dp_r.at[0])
        everyone = lax.dot_general(
            fac[:, 0:width], xs[t], nt, preferred_element_type=jnp.float32
        )
        kept = jnp.where(chosen, everyone, 0.0)
        lrz[0] = jnp.sum(kept.reshape(GROUPS * SLOTS, RANK, rows), axis=0)
        for i in range(1, SIDE):
            send(lrz.at[0], lrz.at[i], lz_s, lz_r, at((i, 0)))

    def low_along_y():
        received(lrz.at[1:], lz_r)
        lry[0] = (lrz[0] + lrz[1]) + (lrz[2] + lrz[3])
        for i in range(1, SIDE):
            send(lry.at[0], lry.at[i], ly_s, ly_r, at((0, i)))

    def low_whole():
        received(lry.at[1:], ly_r)
        received(fac.at[0 : (GROUPS - 1) * block_rows, out_of], dp_r.at[1])
        total = (lry[0] + lry[1]) + (lry[2] + lry[3])
        total = total.astype(jnp.bfloat16).astype(jnp.float32)
        spread = jnp.concatenate([total] * (GROUPS * SLOTS), axis=0)
        low[...] = jnp.transpose(jnp.where(chosen, spread, 0.0)).astype(jnp.bfloat16)
        for j in range(0, units, 256):
            columns = slice(j, min(j + 256, units))
            factors = fac[:, width + columns.start : width + columns.stop]
            extra[:, columns] = jnp.dot(low[...], factors, preferred_element_type=jnp.float32)

    def step(q, level):
        arrived(q, level)
        for o in LEVELS[q, level]:
            forward(q, o)

    def activate(p):
        some = part_rows(p)

        @pl.loop(0, panels)
        def _(j):
            columns = pl.ds(pl.multiple_of(j * 128, 128), 128)
            up_columns = pl.ds(pl.multiple_of(units + j * 128, 128), 128)
            gate = acc[some, columns] * gs[columns].reshape(1, 128)
            up = acc[some, up_columns] * us[columns].reshape(1, 128) + extra[some, columns]
            hid[some, columns] = (gate / (1.0 + jnp.exp(-gate)) * up).astype(jnp.bfloat16)

    def turn(p):
        count = PARTS[p][1]
        base = TENSOR * bases[p]
        for j in range(0, panels, 2):
            wide = min(2, panels - j)
            turned = jnp.dot(
                hid[part_rows(p), :], tv[:, j * 128 : (j + wide) * 128],
                preferred_element_type=jnp.float32,
            ).astype(jnp.bfloat16)
            for k in range(wide):
                gst[pl.ds(base + (j + k) * count, count), :] = turned[:, k * 128 : (k + 1) * 128]
        rest = TENSOR * shares[p] - panels * count
        if rest:
            gst[pl.ds(base + panels * count, rest), :] = jnp.zeros((rest, 128), jnp.bfloat16)

    def share_of(p, index):
        return pl.ds(pl.multiple_of(TENSOR * bases[p] + index * shares[p], 16), shares[p])

    def slot_of_part(p):
        return pl.ds(bases[p], shares[p])

    far_first = OFFSETS[:0:-1]

    def share_out(p):
        for o in far_first:
            peer = at(o)
            send(
                gst.at[share_of(p, peer), :], ra.at[t, slot_of_part(p), :],
                a1_s, a1_r.at[p], peer,
            )
        ra[t, slot_of_part(p), :] = gst[share_of(p, t), :]

    norm = 1.0 / math.sqrt(HIDDEN_UNITS)

    def mix(p):
        received(ra.at[1:, slot_of_part(p), :], a1_r.at[p])

        @pl.loop(0, shares[p] // 16)
        def _(k):
            tile = pl.ds(pl.multiple_of(bases[p] + k * 16, 16), 16)
            terms = [ra[i, tile, :].astype(jnp.float32) for i in range(TENSOR)]
            for bit in range(4):
                mixed = list(terms)
                for i in range(TENSOR):
                    j = i ^ (1 << bit)
                    if i < j:
                        mixed[i] = terms[i] + terms[j]
                        mixed[j] = terms[i] - terms[j]
                terms = mixed
            for i in range(TENSOR):
                rb[i, tile, :] = (terms[i] * norm).astype(jnp.bfloat16)

        for o in far_first:
            peer = at(o)
            send(
                rb.at[peer, slot_of_part(p), :], rot.at[share_of(p, t), :],
                a2_s, a2_r.at[p], peer,
            )
        rot[share_of(p, t), :] = rb[t, slot_of_part(p), :]

    def gather_back(p):
        received(rot.at[0 : (TENSOR - 1) * shares[p], :], a2_r.at[p])
        count = PARTS[p][1]
        for j in range(panels):
            rotc[part_rows(p), j * 128 : (j + 1) * 128] = rot[
                pl.ds(TENSOR * bases[p] + j * count, count), :
            ]

    def collected(q, o):
        total = part[ORDER[o], rows_of(q), :]
        for c in CHILDREN[q, o]:
            total = total + rsr[ORDER[c], rows_of(q), :].astype(jnp.float32)
        return total

    def pass_up(q, o):
        rss[ORDER[o], rows_of(q), :] = collected(q, o).astype(jnp.bfloat16)
        above = parent(q, o)
        hop = (above[0] - o[0], above[1] - o[1])
        send(
            rss.at[ORDER[o], rows_of(q), :], rsr.at[ORDER[o], rows_of(q), :],
            rs_s, rs_r.at[q, level_of(q, o)], at(hop),
        )

    def project(p, offsets):
        some = part_rows(p)
        for o in offsets:
            target = at(o, -1)
            columns = pl.ds(pl.multiple_of(target * width, width), width)
            part[ORDER[o], some, :] = jnp.dot(
                rotc[some, :], wdv[:, columns], preferred_element_type=jnp.float32
            )
            for q in TREES[p]:
                if o != (0, 0) and not CHILDREN[q, o]:
                    pass_up(q, o)

    def climb(p, level):
        for q in TREES[p]:
            received(
                rsr.at[0 : len(LEVELS[q, level + 1]), rows_of(q), :], rs_r.at[q, level + 1]
            )
            for o in LEVELS[q, level]:
                if level == 0:
                    total = collected(q, o) * ds[...].reshape(1, width)
                    out[rows_of(q), :] = total.astype(jnp.bfloat16)
                elif CHILDREN[q, o]:
                    pass_up(q, o)

    everything = pl.ds(0, rows)
    load(0)
    multiply(everything, 0, 1)
    low_partial()
    step(0, 1)
    step(2, 1)
    low_along_y()
    step(1, 1)
    step(3, 1)
    load(1)
    multiply(everything, 1, 4)
    step(0, 2)
    step(2, 2)
    step(1, 2)
    step(3, 2)
    load(2)
    multiply(part_rows(0), 5, 6)
    low_whole()
    table_copy.start()
    wd_copy.start()
    multiply(part_rows(1), 5, 6)
    load(3)
    step(0, 3)
    step(2, 3)
    multiply(part_rows(0), 11, 5)
    activate(0)
    table_copy.wait()
    turn(0)
    share_out(0)
    step(1, 3)
    step(3, 3)
    multiply(part_rows(1), 11, 5)
    activate(1)
    turn(1)
    share_out(1)
    for p in range(len(PARTS)):
        mix(p)
    wd_copy.wait()
    gather_back(0)
    project(0, OFFSETS[::-1])
    gather_back(1)
    project(1, OFFSETS[::-1])
    for level in (2, 1, 0):
        for p in range(len(PARTS)):
            climb(p, level)
    received(xs.at[0 : TENSOR - 1], ag_s)
    received(fac.at[0 : (GROUPS - 1) * block_rows], dp_s)
    received(lrz.at[1:], lz_s)
    received(lry.at[1:], ly_s)
    received(ra.at[1:], a1_s)
    received(ra.at[1:], a2_s)
    received(rss.at[1:], rs_s)


def local(
    tokens,
    gate_weight_codes,
    up_weight_codes,
    down_weight_codes,
    gate_channel_scale,
    up_channel_scale,
    down_channel_scale,
    adapter_input_factors,
    adapter_output_factors,
    group_adapter_lists,
    row_adapter_entry,
):
    rows, width = tokens.shape
    units = gate_weight_codes.shape[1]
    factors = adapter_input_factors.shape[1]
    picked = GROUPS * SLOTS * RANK
    panels = units // 128
    share = sum(share_rows(count, panels) for _, count in PARTS)
    bf16, f32 = jnp.bfloat16, jnp.float32
    table = jnp.asarray(rotation_table(units), bf16)
    hbm = pl.BlockSpec(memory_space=pl.ANY)
    vmem = pl.BlockSpec(memory_space=pltpu.VMEM)
    dma = pltpu.SemaphoreType.DMA
    return pl.pallas_call(
        body,
        out_shape=pltpu.VMEM((rows, width), bf16),
        in_specs=[hbm] * 12,
        out_specs=vmem,
        scratch_shapes=[
            pltpu.VMEM((TENSOR, rows, width), bf16),
            pltpu.VMEM((TENSOR, width, 2 * units), bf16),
            pltpu.VMEM(down_weight_codes.shape, bf16),
            pltpu.VMEM((units, units), bf16),
            pltpu.VMEM((rows, 2 * units), f32),
            pltpu.VMEM((rows, units), bf16),
            pltpu.VMEM((TENSOR * share, 128), bf16),
            pltpu.VMEM((TENSOR, share, 128), bf16),
            pltpu.VMEM((TENSOR, share, 128), bf16),
            pltpu.VMEM((TENSOR * share, 128), bf16),
            pltpu.VMEM((rows, units), bf16),
            pltpu.VMEM((TENSOR, rows, width), f32),
            pltpu.VMEM((TENSOR, rows, width), bf16),
            pltpu.VMEM((TENSOR, rows, width), bf16),
            pltpu.VMEM((width, factors), bf16),
            pltpu.VMEM((units, factors), bf16),
            pltpu.VMEM((picked, width + units), bf16),
            pltpu.VMEM((picked, width + units), bf16),
            pltpu.VMEM((SIDE, RANK, rows), f32),
            pltpu.VMEM((SIDE, RANK, rows), f32),
            pltpu.VMEM((rows, picked), bf16),
            pltpu.VMEM((rows, units), f32),
            pltpu.VMEM(gate_channel_scale.shape, f32),
            pltpu.VMEM(up_channel_scale.shape, f32),
            pltpu.VMEM(down_channel_scale.shape, f32),
            pltpu.SMEM((GROUPS, SLOTS, GROUPS), jnp.int32),
            pltpu.VMEM(row_adapter_entry.shape, jnp.int32),
            dma,
            dma((len(GROUPS_OF_BLOCKS),)),
            dma((9,)),
            dma,
            dma((QUARTERS, SIDE)),
            dma,
            dma((2,)),
            dma,
            dma,
            dma,
            dma,
            dma,
            dma((len(PARTS),)),
            dma,
            dma((len(PARTS),)),
            dma,
            dma((QUARTERS, SIDE)),
        ],
        compiler_params=pltpu.CompilerParams(
            collective_id=0, has_side_effects=True, vmem_limit_bytes=60 * MIB
        ),
    )(
        tokens,
        gate_weight_codes,
        up_weight_codes,
        down_weight_codes,
        gate_channel_scale,
        up_channel_scale,
        down_channel_scale,
        adapter_input_factors,
        adapter_output_factors,
        jnp.transpose(group_adapter_lists, (0, 2, 1)),
        row_adapter_entry,
        table,
    )


def solution(mesh):
    return jax.shard_map(
        local,
        mesh=mesh,
        in_specs=(
            P("dp", "tensor"),
            P(None, "tensor"),
            P(None, "tensor"),
            P("tensor", None),
            P("tensor"),
            P("tensor"),
            P("tensor"),
            P(None, "dp"),
            P("tensor", "dp"),
            P(),
            P("dp"),
        ),
        out_specs=P("dp", "tensor"),
        check_vma=False,
    )
```

```python
import functools
import math

import jax
import jax.numpy as jnp
import numpy as np
from jax import lax
from jax.experimental import pallas as pl
from jax.experimental.pallas import tpu as pltpu
from jax.sharding import PartitionSpec as P

HIDDEN_UNITS = 14336
RANK = 16
SIDE = 4
TENSOR = SIDE * SIDE
GROUPS = 8
SLOTS = 2
QUARTERS = 4
PARTS = ((0, 208), (208, 176))
TREES = ((0, 2), (1, 3))
TREE_ROWS = {0: (0, 96), 2: (96, 112), 1: (208, 96), 3: (304, 80)}
GROUPS_OF_BLOCKS = ((0, 1), (1, 4), (5, 6), (11, 5))
MIB = 1024 * 1024


def steps(a):
    return min(a, SIDE - a)


def depth(o):
    return steps(o[0]) + steps(o[1])


OFFSETS = sorted(((a, b) for a in range(SIDE) for b in range(SIDE)), key=depth)
ORDER = {o: i for i, o in enumerate(OFFSETS)}
NEAR = [o for o in OFFSETS if depth(o) == 1]
OPPOSITE = [(2, 0), (0, 2)]


def parent(q, o):
    dz, dy = o
    via = 1 if q % 2 == 0 else SIDE - 1
    if q < 2:
        return (dz, via if dy == 2 else 0) if dy else (0, 0)
    return (via if dz == 2 else 0, dy) if dz else (0, 0)


def level_of(q, o):
    return 0 if o == (0, 0) else 1 + level_of(q, parent(q, o))


LEVELS = {
    (q, level): [o for o in OFFSETS if level_of(q, o) == level]
    for q in range(QUARTERS)
    for level in range(5)
}
CHILDREN = {
    (q, o): [c for c in OFFSETS if c != (0, 0) and parent(q, c) == o]
    for q in range(QUARTERS)
    for o in OFFSETS
}
for children in CHILDREN.values():
    children.sort(key=depth, reverse=True)


def share_rows(rows, panels):
    return -(-panels * rows // (16 * TENSOR)) * 16


def rotation_table(local_units):
    order = local_units // 28
    index = np.arange(order)
    walsh = np.ones((order, order), np.int64)
    for bit in range(max(order.bit_length() - 1, 0)):
        walsh *= 1 - 2 * ((index[:, None] & index[None, :]) >> bit & 1)
    conference = np.ones((14, 14), np.int64)
    residues = {j * j % 13 for j in range(1, 13)}
    conference[0, 0] = 0
    for i in range(13):
        for j in range(13):
            offset = (j - i) % 13
            conference[i + 1, j + 1] = 0 if offset == 0 else (1 if offset in residues else -1)
    paley = np.kron(conference, np.array([[1, 1], [1, -1]])) + np.kron(
        np.eye(14, dtype=np.int64), np.array([[1, -1], [-1, -1]])
    )
    return np.kron(walsh, paley).astype(np.float32)


def body(
    tokens, wg, wu, wd, gs_in, us_in, ds_in, fa, fb, lists_in, entry_in, table, out,
    xs, wv, wdv, tv, acc, hid, gst, ra, rb, rot, rotc, part, rss, rsr,
    fav, fbv, stage, fac, lrz, lry, low, extra, gs, us, ds, lists, entry,
    own_sem, w_sem, misc_sem, ag_s, ag_r, dp_s, dp_r, lz_s, lz_r, ly_s, ly_r,
    a1_s, a1_r, a2_s, a2_r, rs_s, rs_r,
):
    rows, width = tokens.shape
    units = wg.shape[1]
    panels = units // 128
    shares = [share_rows(count, panels) for _, count in PARTS]
    bases = [sum(shares[:p]) for p in range(len(PARTS))]
    d = lax.axis_index("dp")
    t = lax.axis_index("tensor")
    z = lax.div(t, SIDE)
    y = lax.rem(t, SIDE)

    def at(o, sign=1):
        return (
            lax.rem(z + sign * o[0] + SIDE, SIDE) * SIDE + lax.rem(y + sign * o[1] + SIDE, SIDE)
        )

    def remote(src, dst, send, recv, to, axis="tensor"):
        return pltpu.make_async_remote_copy(
            src_ref=src, dst_ref=dst, send_sem=send, recv_sem=recv,
            device_id={axis: to}, device_id_type=pl.DeviceIdType.MESH,
        )

    def send(*args, **kw):
        remote(*args, **kw).start()

    def received(like, semaphore):
        pltpu.make_async_copy(like, like, semaphore).wait()

    barrier = pltpu.get_barrier_semaphore()
    for o in NEAR + OPPOSITE:
        pl.semaphore_signal(
            barrier, inc=1, device_id={"tensor": at(o)}, device_id_type=pl.DeviceIdType.MESH
        )
    others = [lax.rem(d + i, GROUPS) for i in range(1, GROUPS)]
    for peer in others:
        pl.semaphore_signal(
            barrier, inc=1, device_id={"dp": peer}, device_id_type=pl.DeviceIdType.MESH
        )

    small = [
        pltpu.make_async_copy(src, dst, misc_sem.at[4 + i])
        for i, (src, dst) in enumerate(
            ((lists_in, lists), (entry_in, entry), (gs_in, gs), (us_in, us), (ds_in, ds))
        )
    ]
    small[0].start()
    own = pltpu.make_async_copy(tokens, xs.at[t], own_sem)
    own.start()
    fa_copy = pltpu.make_async_copy(
        fa.at[pl.ds(pl.multiple_of(t * width, width), width), :], fav, misc_sem.at[0]
    )
    fa_copy.start()
    fb_copy = pltpu.make_async_copy(fb, fbv, misc_sem.at[1])
    fb_copy.start()
    for copy in small[1:]:
        copy.start()
    def fetch(group):
        first, count = GROUPS_OF_BLOCKS[group]
        for i in range(first, first + count):
            block = pl.ds(pl.multiple_of(at(OFFSETS[i], -1) * width, width), width)
            pltpu.make_async_copy(wg.at[block, :], wv.at[i, :, 0:units], w_sem.at[group]).start()
            pltpu.make_async_copy(
                wu.at[block, :], wv.at[i, :, units : 2 * units], w_sem.at[group]
            ).start()

    fetch(0)
    fetch(1)
    table_copy = pltpu.make_async_copy(table, tv, misc_sem.at[2])
    wd_copy = pltpu.make_async_copy(wd, wdv, misc_sem.at[3])

    small[0].wait()
    fa_copy.wait()
    fb_copy.wait()
    rank_row = lax.broadcasted_iota(jnp.int32, (RANK, GROUPS * RANK), 0)
    column = lax.broadcasted_iota(jnp.int32, (RANK, GROUPS * RANK), 1)
    picks = []
    for g in range(GROUPS):
        for s in range(SLOTS):
            picked = lists[g, s, d]
            picks.append((column == picked * RANK + rank_row).astype(jnp.float32))
    pick = jnp.concatenate(picks, axis=0).astype(jnp.bfloat16)
    nt = (((1,), (1,)), ((), ()))
    stage[:, 0:width] = lax.dot_general(
        pick, fav[...], nt, preferred_element_type=jnp.float32
    ).astype(jnp.bfloat16)
    stage[:, width:] = lax.dot_general(
        pick, fbv[...], nt, preferred_element_type=jnp.float32
    ).astype(jnp.bfloat16)
    block_rows = SLOTS * RANK
    mine = pl.ds(pl.multiple_of(d * block_rows, block_rows), block_rows)
    fac[mine, :] = stage[mine, :]

    pl.semaphore_wait(barrier, len(NEAR) + len(OPPOSITE) + GROUPS - 1)

    def rows_of(q):
        return pl.ds(*TREE_ROWS[q])

    def part_rows(p):
        return pl.ds(*PARTS[p])

    def forward(q, o):
        source = at(o, -1)
        for c in CHILDREN[q, o]:
            hop = (c[0] - o[0], c[1] - o[1])
            src = tokens.at[rows_of(q), :] if o == (0, 0) else xs.at[source, rows_of(q), :]
            send(
                src, xs.at[source, rows_of(q), :],
                ag_s, ag_r.at[q, level_of(q, c)], at(hop),
            )

    def arrived(q, level):
        received(xs.at[0 : len(LEVELS[q, level]), rows_of(q), :], ag_r.at[q, level])

    def load(group):
        first, count = GROUPS_OF_BLOCKS[group]
        received(wv.at[first : first + count], w_sem.at[group])

    def multiply(some, blocks):
        sources = [at(OFFSETS[i], -1) for i in blocks]
        for n in range(2 * units // 256):
            columns = slice(n * 256, (n + 1) * 256)
            x = jnp.concatenate([xs[source, some, :] for source in sources], axis=1)
            w = jnp.concatenate([wv[i, :, columns] for i in blocks], axis=0)
            product = jnp.dot(x, w, preferred_element_type=jnp.float32)
            if 0 in blocks:
                acc[some, columns] = product
            else:
                acc[some, columns] += product

    def block_of(index):
        return pl.ds(pl.multiple_of(index * block_rows, block_rows), block_rows)

    into, out_of = slice(0, width), slice(width, width + units)
    for peer in others:
        send(
            stage.at[block_of(peer), into], fac.at[mine, into], dp_s, dp_r.at[0], peer, axis="dp"
        )
    for q in TREE_ROWS:
        forward(q, (0, 0))
    for peer in others:
        send(
            stage.at[block_of(peer), out_of], fac.at[mine, out_of],
            dp_s, dp_r.at[1], peer, axis="dp",
        )
    fetch(2)
    fetch(3)

    own.wait()
    for copy in small[1:]:
        copy.wait()

    slot_of = lax.broadcasted_iota(jnp.int32, (GROUPS * SLOTS * RANK, rows), 0) // RANK
    chosen = slot_of == entry[...].reshape(1, rows)

    def low_partial():
        received(fac.at[0 : (GROUPS - 1) * block_rows, into], dp_r.at[0])
        everyone = lax.dot_general(
            fac[:, 0:width], xs[t], nt, preferred_element_type=jnp.float32
        )
        kept = jnp.where(chosen, everyone, 0.0)
        lrz[0] = jnp.sum(kept.reshape(GROUPS * SLOTS, RANK, rows), axis=0)
        for i in range(1, SIDE):
            send(lrz.at[0], lrz.at[i], lz_s, lz_r, at((i, 0)))

    def low_along_y():
        received(lrz.at[1:], lz_r)
        lry[0] = (lrz[0] + lrz[1]) + (lrz[2] + lrz[3])
        for i in range(1, SIDE):
            send(lry.at[0], lry.at[i], ly_s, ly_r, at((0, i)))

    def low_whole():
        received(lry.at[1:], ly_r)
        received(fac.at[0 : (GROUPS - 1) * block_rows, out_of], dp_r.at[1])
        total = (lry[0] + lry[1]) + (lry[2] + lry[3])
        total = total.astype(jnp.bfloat16).astype(jnp.float32)
        spread = jnp.concatenate([total] * (GROUPS * SLOTS), axis=0)
        low[...] = jnp.transpose(jnp.where(chosen, spread, 0.0)).astype(jnp.bfloat16)
        for j in range(0, units, 256):
            columns = slice(j, min(j + 256, units))
            factors = fac[:, width + columns.start : width + columns.stop]
            extra[:, columns] = jnp.dot(low[...], factors, preferred_element_type=jnp.float32)

    def step(q, level):
        arrived(q, level)
        for o in LEVELS[q, level]:
            forward(q, o)

    def last_blocks(p, level):
        for q in TREES[p]:
            multiply(
                rows_of(q),
                [ORDER[o] for o in LEVELS[q, level] if ORDER[o] >= GROUPS_OF_BLOCKS[-1][0]],
            )

    def activate(p):
        some = part_rows(p)

        @pl.loop(0, panels)
        def _(j):
            columns = pl.ds(pl.multiple_of(j * 128, 128), 128)
            up_columns = pl.ds(pl.multiple_of(units + j * 128, 128), 128)
            gate = acc[some, columns] * gs[columns].reshape(1, 128)
            up = acc[some, up_columns] * us[columns].reshape(1, 128) + extra[some, columns]
            hid[some, columns] = (gate / (1.0 + jnp.exp(-gate)) * up).astype(jnp.bfloat16)

    def turn(p):
        count = PARTS[p][1]
        base = TENSOR * bases[p]
        for j in range(0, panels, 2):
            wide = min(2, panels - j)
            turned = jnp.dot(
                hid[part_rows(p), :], tv[:, j * 128 : (j + wide) * 128],
                preferred_element_type=jnp.float32,
            ).astype(jnp.bfloat16)
            for k in range(wide):
                gst[pl.ds(base + (j + k) * count, count), :] = turned[:, k * 128 : (k + 1) * 128]
        rest = TENSOR * shares[p] - panels * count
        if rest:
            gst[pl.ds(base + panels * count, rest), :] = jnp.zeros((rest, 128), jnp.bfloat16)

    def share_of(p, index):
        return pl.ds(pl.multiple_of(TENSOR * bases[p] + index * shares[p], 16), shares[p])

    def slot_of_part(p):
        return pl.ds(bases[p], shares[p])

    far_first = OFFSETS[:0:-1]

    def share_out(p):
        for o in far_first:
            peer = at(o)
            send(
                gst.at[share_of(p, peer), :], ra.at[t, slot_of_part(p), :],
                a1_s, a1_r.at[p], peer,
            )
        ra[t, slot_of_part(p), :] = gst[share_of(p, t), :]

    norm = 1.0 / math.sqrt(HIDDEN_UNITS)

    def mix(p):
        received(ra.at[1:, slot_of_part(p), :], a1_r.at[p])

        @pl.loop(0, shares[p] // 16)
        def _(k):
            tile = pl.ds(pl.multiple_of(bases[p] + k * 16, 16), 16)
            terms = [ra[i, tile, :].astype(jnp.float32) for i in range(TENSOR)]
            for bit in range(4):
                mixed = list(terms)
                for i in range(TENSOR):
                    j = i ^ (1 << bit)
                    if i < j:
                        mixed[i] = terms[i] + terms[j]
                        mixed[j] = terms[i] - terms[j]
                terms = mixed
            for i in range(TENSOR):
                rb[i, tile, :] = (terms[i] * norm).astype(jnp.bfloat16)

        for o in far_first:
            peer = at(o)
            send(
                rb.at[peer, slot_of_part(p), :], rot.at[share_of(p, t), :],
                a2_s, a2_r.at[p], peer,
            )
        rot[share_of(p, t), :] = rb[t, slot_of_part(p), :]

    def gather_back(p):
        received(rot.at[0 : (TENSOR - 1) * shares[p], :], a2_r.at[p])
        count = PARTS[p][1]
        for j in range(panels):
            rotc[part_rows(p), j * 128 : (j + 1) * 128] = rot[
                pl.ds(TENSOR * bases[p] + j * count, count), :
            ]

    def collected(q, o):
        total = part[ORDER[o], rows_of(q), :]
        for c in CHILDREN[q, o]:
            total = total + rsr[ORDER[c], rows_of(q), :].astype(jnp.float32)
        return total

    def pass_up(q, o):
        rss[ORDER[o], rows_of(q), :] = collected(q, o).astype(jnp.bfloat16)
        above = parent(q, o)
        hop = (above[0] - o[0], above[1] - o[1])
        send(
            rss.at[ORDER[o], rows_of(q), :], rsr.at[ORDER[o], rows_of(q), :],
            rs_s, rs_r.at[q, level_of(q, o)], at(hop),
        )

    def project(p, offsets):
        some = part_rows(p)
        for o in offsets:
            target = at(o, -1)
            columns = pl.ds(pl.multiple_of(target * width, width), width)
            part[ORDER[o], some, :] = jnp.dot(
                rotc[some, :], wdv[:, columns], preferred_element_type=jnp.float32
            )
            for q in TREES[p]:
                if o != (0, 0) and not CHILDREN[q, o]:
                    pass_up(q, o)

    def climb(p, level):
        for q in TREES[p]:
            received(
                rsr.at[0 : len(LEVELS[q, level + 1]), rows_of(q), :], rs_r.at[q, level + 1]
            )
            for o in LEVELS[q, level]:
                if level == 0:
                    total = collected(q, o) * ds[...].reshape(1, width)
                    out[rows_of(q), :] = total.astype(jnp.bfloat16)
                elif CHILDREN[q, o]:
                    pass_up(q, o)

    everything = pl.ds(0, rows)
    load(0)
    multiply(everything, range(0, 1))
    low_partial()
    step(0, 1)
    step(2, 1)
    low_along_y()
    step(1, 1)
    step(3, 1)
    load(1)
    multiply(everything, range(1, 5))
    step(0, 2)
    step(2, 2)
    step(1, 2)
    step(3, 2)
    load(2)
    multiply(part_rows(0), range(5, 11))
    low_whole()
    table_copy.start()
    wd_copy.start()
    multiply(part_rows(1), range(5, 11))
    load(3)
    last_blocks(0, 2)
    step(0, 3)
    step(2, 3)
    last_blocks(0, 3)
    activate(0)
    table_copy.wait()
    turn(0)
    share_out(0)
    last_blocks(1, 2)
    step(1, 3)
    step(3, 3)
    last_blocks(1, 3)
    activate(1)
    turn(1)
    share_out(1)
    for p in range(len(PARTS)):
        mix(p)
    wd_copy.wait()
    gather_back(0)
    project(0, OFFSETS[::-1])
    gather_back(1)
    project(1, OFFSETS[::-1])
    for level in (2, 1, 0):
        for p in range(len(PARTS)):
            climb(p, level)
    received(xs.at[0 : TENSOR - 1], ag_s)
    received(fac.at[0 : (GROUPS - 1) * block_rows], dp_s)
    received(lrz.at[1:], lz_s)
    received(lry.at[1:], ly_s)
    received(ra.at[1:], a1_s)
    received(ra.at[1:], a2_s)
    received(rss.at[1:], rs_s)


def local(
    tokens,
    gate_weight_codes,
    up_weight_codes,
    down_weight_codes,
    gate_channel_scale,
    up_channel_scale,
    down_channel_scale,
    adapter_input_factors,
    adapter_output_factors,
    group_adapter_lists,
    row_adapter_entry,
):
    rows, width = tokens.shape
    units = gate_weight_codes.shape[1]
    factors = adapter_input_factors.shape[1]
    picked = GROUPS * SLOTS * RANK
    panels = units // 128
    share = sum(share_rows(count, panels) for _, count in PARTS)
    bf16, f32 = jnp.bfloat16, jnp.float32
    table = jnp.asarray(rotation_table(units), bf16)
    hbm = pl.BlockSpec(memory_space=pl.ANY)
    vmem = pl.BlockSpec(memory_space=pltpu.VMEM)
    dma = pltpu.SemaphoreType.DMA
    return pl.pallas_call(
        body,
        out_shape=pltpu.VMEM((rows, width), bf16),
        in_specs=[hbm] * 12,
        out_specs=vmem,
        scratch_shapes=[
            pltpu.VMEM((TENSOR, rows, width), bf16),
            pltpu.VMEM((TENSOR, width, 2 * units), bf16),
            pltpu.VMEM(down_weight_codes.shape, bf16),
            pltpu.VMEM((units, units), bf16),
            pltpu.VMEM((rows, 2 * units), f32),
            pltpu.VMEM((rows, units), bf16),
            pltpu.VMEM((TENSOR * share, 128), bf16),
            pltpu.VMEM((TENSOR, share, 128), bf16),
            pltpu.VMEM((TENSOR, share, 128), bf16),
            pltpu.VMEM((TENSOR * share, 128), bf16),
            pltpu.VMEM((rows, units), bf16),
            pltpu.VMEM((TENSOR, rows, width), f32),
            pltpu.VMEM((TENSOR, rows, width), bf16),
            pltpu.VMEM((TENSOR, rows, width), bf16),
            pltpu.VMEM((width, factors), bf16),
            pltpu.VMEM((units, factors), bf16),
            pltpu.VMEM((picked, width + units), bf16),
            pltpu.VMEM((picked, width + units), bf16),
            pltpu.VMEM((SIDE, RANK, rows), f32),
            pltpu.VMEM((SIDE, RANK, rows), f32),
            pltpu.VMEM((rows, picked), bf16),
            pltpu.VMEM((rows, units), f32),
            pltpu.VMEM(gate_channel_scale.shape, f32),
            pltpu.VMEM(up_channel_scale.shape, f32),
            pltpu.VMEM(down_channel_scale.shape, f32),
            pltpu.SMEM((GROUPS, SLOTS, GROUPS), jnp.int32),
            pltpu.VMEM(row_adapter_entry.shape, jnp.int32),
            dma,
            dma((len(GROUPS_OF_BLOCKS),)),
            dma((9,)),
            dma,
            dma((QUARTERS, SIDE)),
            dma,
            dma((2,)),
            dma,
            dma,
            dma,
            dma,
            dma,
            dma((len(PARTS),)),
            dma,
            dma((len(PARTS),)),
            dma,
            dma((QUARTERS, SIDE)),
        ],
        compiler_params=pltpu.CompilerParams(
            collective_id=0, has_side_effects=True, vmem_limit_bytes=60 * MIB
        ),
    )(
        tokens,
        gate_weight_codes,
        up_weight_codes,
        down_weight_codes,
        gate_channel_scale,
        up_channel_scale,
        down_channel_scale,
        adapter_input_factors,
        adapter_output_factors,
        jnp.transpose(group_adapter_lists, (0, 2, 1)),
        row_adapter_entry,
        table,
    )


def solution(mesh):
    return jax.shard_map(
        local,
        mesh=mesh,
        in_specs=(
            P("dp", "tensor"),
            P(None, "tensor"),
            P(None, "tensor"),
            P("tensor", None),
            P("tensor"),
            P("tensor"),
            P("tensor"),
            P(None, "dp"),
            P("tensor", "dp"),
            P(),
            P("dp"),
        ),
        out_specs=P("dp", "tensor"),
        check_vma=False,
    )
```
